512 devices in a mesh: gy: 16 (over y, core), gz: 32 (over x, z).
Axes of the slice: x: 4, y: 8, z: 8, core: 2. Of those that a mesh axis runs over, the one named last changes fastest.
Arguments:
- force: float32 [3, 512, 256, 128], P(None, 'gy', 'gz'), may hold values from -6 to 6
- density: float32 [512, 256, 128], P('gy', 'gz'), may hold values from 0.2 to 1
- solid_blocks: int32 [64, 32, 16], P('gy', 'gz'), may hold values from 0 to 1, as said below
- fixed_nodes: int32 [512, 256, 128], P('gy', 'gz'), may hold values 0 or 1
- filter_gain: float32 [256], replicated, may hold values from 0.05 to 1
Outputs:
- displacement: float32 [3, 512, 256, 128], P(None, 'gy', 'gz')
- filtered: float32 [512, 256, 128], P(('gy', 'gz'))
The draws below stay inside these ranges and needn't reach their ends.
Inputs may be any that keep to these rules, and one draw needn't show every extreme that they name: `solid_blocks`: 1 marks a solid block, 0 a void one; the last block along y is solid everywhere.
All inputs are finite; a program needn't handle non-finite values. No bound on the sum of `fixed_nodes` on one device may be relied on, other than what follows from the above.
Results may differ from the reference program's by a relative error of at most 0.0003.
Values sent between devices are 32-bit elements; how exact they have to be, the bound alone decides.
A program may use at most 64 MiB of HBM per device.

```python
import math
import jax
import jax.numpy as jnp
import numpy as np
from jax import lax

CY = 32
X = 128
ITERS = 3
NY = 512
NZ = 256


def draw_solid_blocks(key, part):
    block_rows = jnp.arange(NY // 8, dtype=jnp.int32)[:, None, None]
    picked = jax.random.randint(key, (NY // 8, NZ // 8, X // 8), 0, NY // 8, dtype=jnp.int32)
    return (picked <= block_rows).astype(jnp.int32)


def set_ends(drawn, own_key, least, high):
    longest = drawn.shape.index(max(drawn.shape))
    spots = []
    for shift in (0, 1):
        where = [jax.random.randint(jax.random.fold_in(own_key, axis), (), 0, length) for axis, length in enumerate(drawn.shape)]
        where[longest] = (where[longest] + shift) % drawn.shape[longest]
        spots.append(tuple(where))
    return drawn.at[spots[0]].set(least).at[spots[1]].set(high)


def block_levels(own_key, extent, pieces, least, largest):
    loudness = 1.0
    for dim, blocks in pieces:
        heights = jax.random.uniform(jax.random.fold_in(jax.random.fold_in(own_key, 6), dim), (blocks,), jnp.float32, least / len(pieces), largest / len(pieces))
        loudness = loudness * jnp.repeat(jnp.exp(heights), extent[dim] // blocks).reshape((-1,) + (1,) * (len(extent) - 1 - dim))
    return loudness


def gaussian(stream_key, shape, spread, reach, shards=(), held_as=jnp.bfloat16):
    result = spread * jax.random.normal(stream_key, shape, jnp.float32)
    if shards:
        result = result * block_levels(stream_key, shape, shards, -0.22, 0.18)
    return jnp.clip(result, -reach, reach).astype(held_as)


def setup_inputs(seed: int = 0) -> dict:
    splits = jax.random.split(jax.random.key(seed), 6)
    force = gaussian(splits[0], (3, NY, NZ, X), 1.0, 6.0, ((1, 16), (2, 32)), jnp.float32)
    density = jnp.clip(0.2 + 0.8 * jax.random.uniform(splits[1], (NY, NZ, X), jnp.float32) ** block_levels(splits[1], (NY, NZ, X), ((0, 16), (1, 32)), -0.2, 0.2), 0.2, 1.0)
    solid_blocks = draw_solid_blocks(jax.random.fold_in(splits[5], 71), 0)
    fixed_nodes = set_ends((jax.random.randint(splits[3], (NY, NZ, X), 0, 8) < 1).astype(jnp.int32), jax.random.fold_in(splits[3], 1), 0, 1)
    filter_gain = jnp.clip(jnp.exp(jax.random.uniform(splits[4], (NZ,), jnp.float32, math.log(0.05), math.log(1.0))), 0.05, 1.0)
    return dict(force=force, density=density, solid_blocks=solid_blocks, fixed_nodes=fixed_nodes, filter_gain=filter_gain)


MIN_MODULUS = 0.1
DIAG_FLOOR = 0.5
CORNERS = [(a, b, c) for a in (0, 1) for b in (0, 1) for c in (0, 1)]
HIGHEST = lax.Precision.HIGHEST

def element_matrix():
    poisson = 0.3
    lame_first = poisson / ((1.0 + poisson) * (1.0 - 2.0 * poisson))
    shear_modulus = 1.0 / (2.0 * (1.0 + poisson))
    elastic = np.zeros((6, 6))
    elastic[:3, :3] = lame_first
    for axis in range(3):
        elastic[axis, axis] = lame_first + 2.0 * shear_modulus
        elastic[3 + axis, 3 + axis] = shear_modulus
    gauss_points = [0.5 - 0.5 / np.sqrt(3.0), 0.5 + 0.5 / np.sqrt(3.0)]
    stiffness = np.zeros((24, 24))
    for first in gauss_points:
        for second in gauss_points:
            for third in gauss_points:
                location = (first, second, third)
                strain = np.zeros((6, 24))
                for corner, corner_bits in enumerate(CORNERS):
                    gradient = []
                    for axis in range(3):
                        amount = 1.0
                        for other in range(3):
                            if other == axis:
                                amount *= 1.0 if corner_bits[other] else -1.0
                            else:
                                amount *= location[other] if corner_bits[other] else 1.0 - location[other]
                        gradient.append(amount)
                    column = 3 * corner
                    strain[0, column] = gradient[0]
                    strain[1, column + 1] = gradient[1]
                    strain[2, column + 2] = gradient[2]
                    strain[3, column] = gradient[1]
                    strain[3, column + 1] = gradient[0]
                    strain[4, column + 1] = gradient[2]
                    strain[4, column + 2] = gradient[1]
                    strain[5, column] = gradient[2]
                    strain[5, column + 2] = gradient[0]
                stiffness += strain.T @ elastic @ strain / 8.0
    return stiffness

def corner_sum(corner_forces, rows_y, cols_z, depth):
    total = None
    for corner, (a, b, c) in enumerate(CORNERS):
        term = corner_forces[3 * corner:3 * corner + 3, 1 - a:1 - a + rows_y, 1 - b:1 - b + cols_z, 1 - c:1 - c + depth]
        total = term if total is None else total + term
    return total

def region_moduli(mod_halo):
    rows_y = mod_halo.shape[0] - 2
    cols_z = mod_halo.shape[1] - 2
    depth = mod_halo.shape[2]
    padded_mod = jnp.pad(mod_halo, ((0, 0), (0, 0), (1, 0)))
    return padded_mod[:rows_y + 1, :cols_z + 1, :depth + 1]

def node_forces(node_halo, mod_halo, stiffness):
    rows_y = node_halo.shape[1] - 2
    cols_z = node_halo.shape[2] - 2
    depth = node_halo.shape[3]
    padded = jnp.pad(node_halo, ((0, 0), (0, 0), (0, 0), (1, 1)))
    corner_values = jnp.concatenate([padded[:, a:a + rows_y + 1, b:b + cols_z + 1, c:c + depth + 1] for a, b, c in CORNERS], axis=0)
    corner_forces = region_moduli(mod_halo)[None] * jnp.einsum('pq,qyzx->pyzx', stiffness, corner_values, precision=HIGHEST)
    return corner_sum(corner_forces, rows_y, cols_z, depth)

def node_diag(mod_halo, stiff_diag):
    rows_y = mod_halo.shape[0] - 2
    cols_z = mod_halo.shape[1] - 2
    depth = mod_halo.shape[2]
    corner_forces = region_moduli(mod_halo)[None] * stiff_diag[:, None, None, None]
    return corner_sum(corner_forces, rows_y, cols_z, depth)

def owned_energy(upper_nodes, stiffness):
    rows_y = upper_nodes.shape[1] - 1
    cols_z = upper_nodes.shape[2] - 1
    depth = upper_nodes.shape[3]
    padded = jnp.pad(upper_nodes, ((0, 0), (0, 0), (0, 0), (0, 1)))
    corner_values = jnp.concatenate([padded[:, a:a + rows_y, b:b + cols_z, c:c + depth] for a, b, c in CORNERS], axis=0)
    applied = jnp.einsum('pq,qyzx->pyzx', stiffness, corner_values, precision=HIGHEST)
    return lax.optimization_barrier(jnp.sum(corner_values * applied, axis=0))

def reference(force, density, solid_blocks, fixed_nodes, filter_gain):
    stiffness = jnp.asarray(element_matrix(), jnp.float32)
    stiff_diag = jnp.diagonal(stiffness)
    solid = jnp.repeat(jnp.repeat(jnp.repeat(solid_blocks, 8, axis=0), 8, axis=1), 8, axis=2).astype(jnp.float32)
    modulus = solid * (MIN_MODULUS + (1.0 - MIN_MODULUS) * density ** 3)
    free = (1 - fixed_nodes).astype(jnp.float32)[None]
    mod_pad = jnp.pad(modulus, ((1, 1), (1, 1), (0, 0)))
    slabs = jnp.arange(NY // CY, dtype=jnp.int32)
    zero = jnp.int32(0)

    def mod_slab(index):
        return lax.dynamic_slice(mod_pad, (index * CY, zero, zero), (CY + 2, NZ + 2, X))

    def join(stacked):
        return jnp.moveaxis(stacked, 0, 1).reshape(3, NY, NZ, X)
    diag = join(lax.map(lambda index: node_diag(mod_slab(index), stiff_diag), slabs))
    inverse = 1.0 / jnp.maximum(diag, DIAG_FLOOR)

    def apply(direction):
        masked = jnp.pad(free * direction, ((0, 0), (1, 1), (1, 1), (0, 0)))

        def slab_force(index):
            node_halo = lax.dynamic_slice(masked, (zero, index * CY, zero, zero), (3, CY + 2, NZ + 2, X))
            return node_forces(node_halo, mod_slab(index), stiffness)
        return free * join(lax.map(slab_force, slabs)) + (1.0 - free) * direction
    displacement = jnp.zeros_like(force)
    residual = free * force
    precond = inverse * residual
    direction = precond
    rz_now = jnp.sum(residual * precond)
    for step in range(ITERS):
        image = apply(direction)
        alpha = rz_now / jnp.sum(direction * image)
        displacement = displacement + alpha * direction
        residual = residual - alpha * image
        precond = inverse * residual
        rz_next = jnp.sum(residual * precond)
        direction = precond + rz_next / rz_now * direction
        rz_now = rz_next
    disp_pad = jnp.pad(displacement, ((0, 0), (0, 1), (0, 1), (0, 0)))

    def slab_energy(index):
        upper_nodes = lax.dynamic_slice(disp_pad, (zero, index * CY, zero, zero), (3, CY + 1, NZ + 1, X))
        return owned_energy(upper_nodes, stiffness)
    energy = lax.map(slab_energy, slabs).reshape(NY, NZ, X)
    sensitivity = -3.0 * (1.0 - MIN_MODULUS) * density ** 2 * solid * energy
    weighted = density * sensitivity
    spectrum = jnp.fft.fft(weighted, axis=1) * filter_gain[None, :, None]
    filtered = jnp.real(jnp.fft.ifft(spectrum, axis=1)) / density
    return (displacement, filtered.astype(jnp.float32))
```

```python
import functools

import jax
import jax.numpy as jnp
import numpy as np
from jax import lax
from jax.experimental import pallas as pl
from jax.experimental.pallas import tpu as pltpu
from jax.sharding import PartitionSpec as P

MIN_MODULUS = 0.1
DIAG_FLOOR = 0.5
POISSON = 0.3
SHEAR = 1.0 / (2.0 * (1.0 + POISSON))
LAME = POISSON / ((1.0 + POISSON) * (1.0 - 2.0 * POISSON))
UNIT = SHEAR / 16.0
VOLUME = 0.5 * LAME / SHEAR
BEND = LAME / (3.0 * SHEAR)
TWIST = 1.0 / 3.0
WARP = (LAME + 4.0 * SHEAR) / 9.0 / SHEAR
KE_DIAG = (LAME + 4.0 * SHEAR) / 9.0
SHIFT = 1.0
PLANE = 16
FAR = 656
F32 = jnp.float32
HIGHEST = lax.Precision.HIGHEST
STEPS = [(-1, 0), (1, 0), (0, -1), (0, 1), (-1, -1), (-1, 1), (1, -1), (1, 1)]
LOWERS = (0, 2, 4)


def stress(y, z, x, m):
    m2, m3, m4 = 2.0 * m, TWIST * m, WARP * m
    gy, gz, gx = {}, {}, {}
    bulk = VOLUME * (y["100"] + z["010"] + x["001"])
    gy["100"] = m2 * (y["100"] + bulk)
    gz["010"] = m2 * (z["010"] + bulk)
    gx["001"] = m2 * (x["001"] + bulk)
    gy["010"] = gz["100"] = m * (y["010"] + z["100"])
    gz["001"] = gx["010"] = m * (z["001"] + x["010"])
    gy["001"] = gx["100"] = m * (y["001"] + x["100"])
    bend = BEND * (z["110"] + x["101"])
    gz["110"], gx["101"] = m * (z["110"] + bend), m * (x["101"] + bend)
    bend = BEND * (y["110"] + x["011"])
    gy["110"], gx["011"] = m * (y["110"] + bend), m * (x["011"] + bend)
    bend = BEND * (y["101"] + z["011"])
    gy["101"], gz["011"] = m * (y["101"] + bend), m * (z["011"] + bend)
    twist = y["011"] + z["101"] + x["110"]
    gy["011"] = m3 * (y["011"] + twist)
    gz["101"] = m3 * (z["101"] + twist)
    gx["110"] = m3 * (x["110"] + twist)
    gy["111"], gz["111"], gx["111"] = m4 * y["111"], m4 * z["111"], m4 * x["111"]
    return gy, gz, gx


def energy_of(coefs):
    total = None
    for c, g in zip(coefs, stress(*coefs, 1.0)):
        for key in g:
            term = c[key] * g[key]
            total = term if total is None else total + term
    return total


def pair_y(low, high):
    coefs = []
    for a, b in zip(low, high):
        c = {}
        for key in a:
            if key != "00":
                c["0" + key] = a[key] + b[key]
            c["1" + key] = b[key] - a[key]
        coefs.append(c)
    return coefs


def spread_y(g):
    low, high = {}, {}
    for key in ("00", "01", "10", "11"):
        d = g["1" + key]
        if key == "00":
            low[key], high[key] = -d, d
        else:
            s = g["0" + key]
            low[key], high[key] = s - d, s + d
    return low, high


def kernel(
    ny, nz, lines,
    force_h, dens_h, solid_h, fixed_h, gain_h, cos_h, sin_h,
    disp_h, filt_h,
    force, dens, solid, fixed, gain, cosine, sine,
    mod, mod_low, mod_stage, mod_face, mod_edge,
    inv, r0, w0, w1, v0, v1, v2, vx, low_z, low_zx,
    a_low, b_low, a_up, b_up, p_low, p_up, q_low, q_up,
    stage_z, stage_c, land_y, land_z, land_c,
    tmp, sums, acc, slots_y, slots_z,
    circ, weighted, line_w, line_d, disp, filt,
    load_sem, store_sem, mod_send, mod_recv, halo_send, halo_recv, sum_send, sum_recv, line_send, line_recv,
):
    iy, iz = lax.axis_index("gy"), lax.axis_index("gz")
    lane = lax.broadcasted_iota(jnp.int32, (8, 128), 1)
    first_lane, last_lane = lane == 0, lane == 127
    zeros = jnp.zeros((8, 128), F32)

    def at_upper(u):
        return jnp.where(last_lane, 0.0, pltpu.roll(u, 127, 1))

    def from_lower(u):
        return jnp.where(first_lane, 0.0, pltpu.roll(u, 1, 1))

    def modulus(e):
        return mod[pl.ds(8 * e if isinstance(e, int) else pl.multiple_of(8 * e, 8), 8), :]

    loads = [
        pltpu.make_async_copy(src, dst, load_sem.at[i])
        for i, (src, dst) in enumerate(
            [(dens_h, dens), (solid_h, solid), (fixed_h, fixed), (force_h, force), (gain_h, gain), (cos_h, cosine), (sin_h, sine)]
        )
    ]
    for load in loads:
        load.start()

    barrier = pltpu.get_barrier_semaphore()

    def greet_z(i, carry):
        pl.semaphore_signal(barrier, 1, device_id={"gz": lax.rem(iz + i, nz)})
        return carry

    def greet_y(i, carry):
        pl.semaphore_signal(barrier, 1, device_id={"gy": lax.rem(iy + i, ny)})
        return carry

    lax.fori_loop(1, nz, greet_z, 0)
    lax.fori_loop(1, ny, greet_y, 0)

    def there(step):
        sy, sz = step
        ok = None
        for index, s, n in ((iy, sy, ny), (iz, sz, nz)):
            if s:
                here = index >= 1 if s < 0 else index < n - 1
                ok = here if ok is None else jnp.logical_and(ok, here)
        return ok

    def device(step):
        return {"gy": iy + step[0], "gz": iz + step[1]}

    for sy, sz in STEPS[4:]:
        pl.semaphore_signal(barrier, 1, device_id={"gy": lax.rem(iy + sy + ny, ny), "gz": lax.rem(iz + sz + nz, nz)})

    loads[0].wait()
    loads[1].wait()
    flags = solid[:, 0, :].astype(F32)
    spread = (
        lax.broadcasted_iota(jnp.int32, (16, 128), 1) // 8 == lax.broadcasted_iota(jnp.int32, (16, 128), 0)
    ).astype(F32)
    solid_rows = jnp.dot(flags, spread, precision=HIGHEST, preferred_element_type=F32)
    for block in range(4):
        row = solid_rows[block : block + 1]
        for y in range(8 * block, 8 * block + 8):
            d = dens[y]
            mod[pl.ds(8 * (y + 1), 8), :] = row * (UNIT * MIN_MODULUS + (UNIT * (1.0 - MIN_MODULUS)) * (d * d * d))
    for j in range(4):
        mod_stage[pl.ds(8 * j, 8), :] = mod[pl.ds(8 * (8 * j + 1) + 7, 8, 8), :]

    pl.semaphore_wait(barrier, nz - 1 + ny - 1 + 4)

    mod_copies = []
    for i, (step, src, dst) in enumerate(
        [((1, 0), mod.at[pl.ds(256, 8)], mod.at[pl.ds(0, 8)]), ((0, 1), mod_stage, mod_face), ((1, 1), mod_stage.at[pl.ds(24, 8)], mod_edge)]
    ):
        down = (-step[0], -step[1])
        mod_copies.append((step, down, pltpu.make_async_remote_copy(
            src, dst, mod_send.at[i], mod_recv.at[i], device_id=device(step))))

    for step, down, copy in mod_copies:
        @pl.when(there(step))
        def _(copy=copy):
            copy.start()

    for (step, down, copy), fill in zip(mod_copies, (mod.at[pl.ds(0, 8)], mod_face, mod_edge)):
        @pl.when(jnp.logical_not(there(down)))
        def _(fill=fill):
            fill[...] = jnp.zeros(fill.shape, F32)

    def send_density(i, carry):
        to = lax.rem(iz + i, nz)
        pltpu.make_async_remote_copy(
            dens.at[pl.ds(to * lines, lines)], line_d.at[:, pl.ds(pl.multiple_of(iz * 8, 8), 8), :],
            line_send.at[0], line_recv.at[0], device_id={"gz": to},
        ).start()
        return carry

    lax.fori_loop(1, nz, send_density, 0)
    for i in range(lines):
        line_d[i, pl.ds(pl.multiple_of(iz * 8, 8), 8), :] = dens[iz * lines + i]

    for load in loads[4:]:
        load.wait()
    length = cosine.shape[0]
    gains = gain[...] * (1.0 / length)
    circ[...] = jnp.dot(cosine[...] * gains, cosine[...], precision=HIGHEST, preferred_element_type=F32) + jnp.dot(
        sine[...] * gains, sine[...], precision=HIGHEST, preferred_element_type=F32)

    loads[2].wait()
    loads[3].wait()

    def halo_copies(k, src, which):
        copies = []
        for i in which:
            sy, sz = STEPS[i]
            if sz == 0:
                s, d = src.at[:, pl.ds(PLANE * (1 if sy < 0 else 32), 8), :], land_y.at[k, i]
            elif sy == 0:
                s, d = stage_z.at[k, i - 2], land_z.at[k, i - 2]
            else:
                s, d = stage_c.at[k, i - 4], land_c.at[k, i - 4]
            copies.append((i, pltpu.make_async_remote_copy(
                s, d, halo_send.at[k, i], halo_recv.at[k, i], device_id=device(STEPS[i]))))
        return copies

    def send_halo(k, src, which):
        for c in range(3):
            for side, z in ((0, 0), (1, 7)):
                if side + 2 in which:
                    for j in range(4):
                        stage_z[k, side, c, pl.ds(8 * j, 8), :] = src[c, pl.ds(PLANE * (8 * j + 1) + z, 8, PLANE), :]
            for i in which:
                if i >= 4:
                    row = PLANE * (1 if STEPS[i][0] < 0 else 32) + (0 if STEPS[i][1] < 0 else 7)
                    stage_c[k, i - 4, pl.ds(c, 1), :] = src[c, pl.ds(row, 1), :]
        for i, copy in halo_copies(k, src, which):
            @pl.when(there(STEPS[i]))
            def _(copy=copy):
                copy.start()

    def land_of(k, i):
        return land_y.at[k, i] if i < 2 else land_z.at[k, i - 2] if i < 4 else land_c.at[k, i - 4]

    def clear_halo(k, which):
        for i in which:
            @pl.when(jnp.logical_not(there((-STEPS[i][0], -STEPS[i][1]))))
            def _(i=i):
                ref = land_of(k, i)
                ref[...] = jnp.zeros(ref.shape, F32)

    def wait_halo(k, src, which):
        for i, copy in halo_copies(k, src, which):
            @pl.when(there((-STEPS[i][0], -STEPS[i][1])))
            def _(copy=copy):
                copy.wait_recv()

    def wait_sent(k, src, which):
        for i, copy in halo_copies(k, src, which):
            @pl.when(there(STEPS[i]))
            def _(copy=copy):
                copy.wait_send()

    def put(ref, rows, u):
        ref[rows] = u
        vx[rows] = at_upper(u)

    def place_halo(k, ref, which):
        for c in range(3):
            put(ref, (c, pl.ds(PLANE * 33, 8), slice(None)), land_y[k, 0, c])
            if 1 in which:
                put(ref, (c, pl.ds(0, 8), slice(None)), land_y[k, 1, c])
            for j in range(4):
                rows = (c, pl.ds(PLANE * (8 * j + 1) + 8, 8, PLANE), slice(None))
                put(ref, rows, land_z[k, 0, c, pl.ds(8 * j, 8), :])
                if 3 in which:
                    u = land_z[k, 1, c, pl.ds(8 * j, 8), :]
                    low_z[c, pl.ds(8 * j + 1, 8), :] = u
                    low_zx[c, pl.ds(8 * j + 1, 8), :] = at_upper(u)
        for i in which:
            if i < 4:
                continue
            u = land_c[k, i - 4]
            ux = at_upper(u)
            y_row = 33 if STEPS[i][0] < 0 else 0
            for c in range(3):
                if STEPS[i][1] < 0:
                    ref[c, pl.ds(PLANE * y_row + 8, 1), :] = u[c : c + 1]
                    vx[c, pl.ds(PLANE * y_row + 8, 1), :] = ux[c : c + 1]
                else:
                    low_z[c, pl.ds(y_row, 1), :] = u[c : c + 1]
                    low_zx[c, pl.ds(y_row, 1), :] = ux[c : c + 1]

    def pair_zx(u0, x0, u1, x1):
        s0, d0, s1, d1 = u0 + x0, x0 - u0, u1 + x1, x1 - u1
        return {"00": s0 + s1, "01": d0 + d1, "10": s1 - s0, "11": d1 - d0}

    def plane(ref, row):
        row = pl.multiple_of(row, PLANE)
        return [
            pair_zx(ref[c, pl.ds(row, 8), :], vx[c, pl.ds(row, 8), :], ref[c, pl.ds(row + 1, 8), :], vx[c, pl.ds(row + 1, 8), :])
            for c in range(3)
        ]

    def low_layer(ref):
        for j in range(5):
            def rows(start):
                return [
                    pair_zx(
                        low_z[c, pl.ds(start, 8), :], low_zx[c, pl.ds(start, 8), :],
                        ref[c, pl.ds(PLANE * start, 8, PLANE), :], vx[c, pl.ds(PLANE * start, 8, PLANE), :])
                    for c in range(3)
                ]
            coefs = pair_y(rows(8 * j), rows(8 * j + 1))
            for c, g in enumerate(stress(*coefs, mod_low[pl.ds(8 * j, 8), :])):
                for part, start, pa, pb in zip(spread_y(g), (8 * j, 8 * j + 1), (p_low, p_up), (q_low, q_up)):
                    s, d = part["00"] + part["10"], part["01"] + part["11"]
                    pa[c, pl.ds(start, 8), :] = s - d
                    pb[c, pl.ds(start, 8), :] = s + d
        for c in range(3):
            for j in range(4):
                rows = pl.ds(8 * j + 1, 8)
                to = (c, pl.ds(PLANE * 8 * j, 8, PLANE), slice(None))
                a_up[to] = p_low[c, rows, :] + p_up[c, rows, :]
                b_up[to] = q_low[c, rows, :] + q_up[c, rows, :]

    def flat(planes):
        return tuple(p[key] for p in planes for key in ("00", "01", "10", "11"))

    def unflat(values):
        keys = ("00", "01", "10", "11")
        return [dict(zip(keys, values[4 * c : 4 * c + 4])) for c in range(3)]

    def forces(ref):
        low, high = plane(ref, 0), plane(ref, PLANE)
        upper = [spread_y(g)[1] for g in stress(*pair_y(low, high), modulus(0))]

        def one(e, low, upper):
            high = plane(ref, PLANE * (e + 1))
            new = []
            for c, g in enumerate(stress(*pair_y(low, high), modulus(e))):
                lo, hi = spread_y(g)
                t = {key: upper[c][key] + lo[key] for key in lo}
                new.append(hi)
                sa, sb, da, db = t["00"] - t["01"], t["00"] + t["01"], t["10"] - t["11"], t["10"] + t["11"]
                row = pl.multiple_of(PLANE * (e - 1), PLANE)
                a_low[c, e - 1] = sa - da
                b_low[c, e - 1] = sb - db
                a_up[c, pl.ds(row + 1, 8), :] = sa + da
                b_up[c, pl.ds(row + 1, 8), :] = sb + db
            return high, new

        def body(i, carry):
            low, upper = unflat(carry[:12]), unflat(carry[12:])
            for k in range(4):
                low, upper = one(4 * i + 1 + k, low, upper)
            return flat(low) + flat(upper)

        lax.fori_loop(0, 8, body, flat(high) + flat(upper))

    def finish(ref, image, after):
        def body(i, carry):
            for k in range(4):
                y = 4 * i + k
                held = fixed[y] != 0
                scale = inv[y]
                row = pl.multiple_of(PLANE * y, PLANE)
                for c in range(3):
                    f = (a_low[c, y] + a_up[c, pl.ds(row, 8), :]) + from_lower(b_low[c, y] + b_up[c, pl.ds(row, 8), :])
                    v = ref[c, pl.ds(row + PLANE, 8), :]
                    w = jnp.where(held, v, f)
                    image[c, y] = w
                    new = scale * w - SHIFT * v
                    after[c, pl.ds(row + PLANE, 8), :] = new
                    vx[c, pl.ds(row + PLANE, 8), :] = at_upper(new)
            return carry
        lax.fori_loop(0, 8, body, 0)

    def dots(pairs):
        def get(ref, c, y):
            if ref.shape[1] == FAR:
                return ref[c, pl.ds(pl.multiple_of(PLANE * y + PLANE, PLANE), 8), :]
            return ref[c, y]

        def body(i, carry):
            carry = list(carry)
            for k in range(2):
                for c in range(3):
                    held = {}
                    for p, (slot, a, b) in enumerate(pairs):
                        for ref in (a, b):
                            if id(ref) not in held:
                                held[id(ref)] = get(ref, c, 2 * i + k)
                        carry[p] = carry[p] + held[id(a)] * held[id(b)]
            return tuple(carry)

        total = lax.fori_loop(0, 16, body, (zeros,) * len(pairs))
        for (slot, a, b), t in zip(pairs, total):
            acc[pl.ds(slot, 1), :] = jnp.sum(t, axis=0, keepdims=True)

    for c in range(3):
        def body(i, carry, c=c):
            for k in range(4):
                y = 4 * i + k
                r0[c, y] = jnp.where(fixed[y] != 0, 0.0, force[c, y])
            return carry
        lax.fori_loop(0, 8, body, 0)
    every = tuple(range(8))
    clear_halo(0, every)
    clear_halo(1, every)
    clear_halo(2, LOWERS)
    acc[...] = jnp.zeros(acc.shape, F32)

    for step, down, copy in mod_copies:
        @pl.when(there(down))
        def _(copy=copy):
            copy.wait_recv()

    for j in range(4):
        mod_low[pl.ds(8 * j + 1, 8), :] = mod_face[pl.ds(8 * j, 8), :]
    mod_low[pl.ds(0, 1), :] = mod_edge[pl.ds(7, 1), :]
    for j in range(4):
        tmp[pl.ds(PLANE * 8 * j, 8, PLANE), :] = mod_low[pl.ds(8 * j, 8), :] + mod_low[pl.ds(8 * j + 1, 8), :]

    def sum_moduli(i, carry):
        for k in range(4):
            y = 4 * i + k
            t = modulus(y) + modulus(y + 1)
            sums[y] = t
            tmp[pl.ds(pl.multiple_of(PLANE * y, PLANE) + 1, 8), :] = t
        return carry
    lax.fori_loop(0, 8, sum_moduli, 0)

    def start(i, carry):
        for k in range(4):
            y = 4 * i + k
            t = sums[y] + tmp[pl.ds(pl.multiple_of(PLANE * y, PLANE), 8), :]
            t = t + from_lower(t)
            scale = 1.0 / jnp.maximum((KE_DIAG / UNIT) * t, DIAG_FLOOR)
            inv[y] = scale
            row = pl.multiple_of(PLANE * y + PLANE, PLANE)
            for c in range(3):
                v = scale * r0[c, y]
                v0[c, pl.ds(row, 8), :] = v
                vx[c, pl.ds(row, 8), :] = at_upper(v)
        return carry
    lax.fori_loop(0, 8, start, 0)

    send_halo(0, v0, every)
    dots([(0, r0, v0)])
    wait_halo(0, v0, every)
    place_halo(0, v0, every)
    low_layer(v0)
    forces(v0)
    finish(v0, w0, v1)
    send_halo(1, v1, every)
    dots([(1, r0, v1), (3, v0, w0), (4, v1, w0)])
    wait_halo(1, v1, every)
    place_halo(1, v1, every)
    low_layer(v1)
    forces(v1)
    finish(v1, w1, v2)
    send_halo(2, v2, LOWERS)
    dots([(2, r0, v2), (5, v2, w0), (6, v1, w1), (7, v2, w1)])
    wait_halo(2, v2, LOWERS)
    place_halo(2, v2, LOWERS)
    wait_sent(0, v0, every)

    def stored_energy(i, carry):
        low, total = unflat(carry[:12]), carry[12]
        for k in range(4):
            e = 4 * i + 1 + k
            high = plane(v2, PLANE * (e + 1))
            total = total + modulus(e) * energy_of(pair_y(low, high))
            low = high
        return flat(low) + (total,)
    total = lax.fori_loop(0, 8, stored_energy, flat(plane(v2, PLANE)) + (zeros,))[12]
    acc[pl.ds(8, 1), :] = jnp.sum(total, axis=0, keepdims=True)

    column = jnp.sum(acc[...], axis=1, keepdims=True)
    rows = lax.broadcasted_iota(jnp.int32, (16, 128), 0)
    lanes = lax.broadcasted_iota(jnp.int32, (16, 128), 1)
    part = jnp.sum(jnp.where(rows == lanes, column, 0.0), axis=0, keepdims=True)
    for k, (axis, me, n, slots) in enumerate((("gy", iy, ny, slots_y), ("gz", iz, nz, slots_z))):
        slots[me] = part

        def send_sum(i, carry, k=k, axis=axis, me=me, n=n, slots=slots):
            pltpu.make_async_remote_copy(
                slots.at[me], slots.at[me], sum_send.at[k], sum_recv.at[k], device_id={axis: lax.rem(me + i, n)},
            ).start()
            return carry
        lax.fori_loop(1, n, send_sum, 0)
        whole = slots.at[pl.ds(0, n - 1)]
        pltpu.make_async_copy(whole, whole, sum_recv.at[k]).wait()
        part = jnp.sum(slots[:, 0, :], axis=0, keepdims=True)

    lane1 = lax.broadcasted_iota(jnp.int32, (1, 128), 1)

    def entry(i):
        return jnp.sum(jnp.where(lane1 == i, part, 0.0), axis=1, keepdims=True)

    b0, b1, b2, g00, g10, g20, g11, g21, g22 = (entry(i) for i in range(9))
    l10, l20 = g10 / g00, g20 / g00
    d1 = g11 - l10 * g10
    e21 = g21 - l20 * g10
    l21 = e21 / d1
    d2 = g22 - l20 * g20 - l21 * e21
    y1 = b1 - l10 * b0
    y2 = b2 - l20 * b0 - l21 * y1
    c2 = y2 / d2
    c1 = y1 / d1 - l21 * c2
    c0 = b0 / g00 - l10 * c1 - l20 * c2
    c0, c1, c2 = (jnp.broadcast_to(c, (8, 128)) for c in (c0, c1, c2))

    def combine(yy, c, off):
        rows = (c, pl.ds(pl.multiple_of(PLANE * yy, PLANE) + off, 8), slice(None))
        u = c0 * v0[rows] + c1 * v1[rows] + c2 * v2[rows]
        v0[rows] = u
        vx[rows] = at_upper(u)
        return u

    def displace(i, carry):
        for k in range(4):
            for c in range(3):
                disp[c, 4 * i + k] = combine(4 * i + k + 1, c, 0)
                combine(4 * i + k + 1, c, 8)
        return carry
    lax.fori_loop(0, 8, displace, 0)
    for c in range(3):
        combine(33, c, 0)
        combine(33, c, 8)
    disp_copy = pltpu.make_async_copy(disp, disp_h, store_sem.at[0])
    disp_copy.start()

    solid_scale = (-3.0 * (1.0 - MIN_MODULUS) * UNIT) * solid_rows

    def sensitivities(block):
        def body(i, carry):
            low = unflat(carry)
            for k in range(4):
                y = 8 * block + 4 * i + k
                high = plane(v0, PLANE * (y + 2))
                d = dens[y]
                weighted[y] = (solid_scale[block : block + 1] * (d * d * d)) * energy_of(pair_y(low, high))
                low = high
            return flat(low)
        return body
    carry = flat(plane(v0, PLANE))
    for block in range(4):
        carry = lax.fori_loop(0, 2, sensitivities(block), carry)

    def send_weighted(i, carry):
        to = lax.rem(iz + i, nz)
        pltpu.make_async_remote_copy(
            weighted.at[pl.ds(to * lines, lines)], line_w.at[:, pl.ds(pl.multiple_of(iz * 8, 8), 8), :],
            line_send.at[1], line_recv.at[1], device_id={"gz": to},
        ).start()
        return carry
    lax.fori_loop(1, nz, send_weighted, 0)
    for i in range(lines):
        line_w[i, pl.ds(pl.multiple_of(iz * 8, 8), 8), :] = weighted[iz * lines + i]

    others = [ref.at[:, pl.ds(0, 8 * (nz - 1)), :] for ref in (line_d, line_w)]
    for k in range(2):
        pltpu.make_async_copy(others[k], others[k], line_recv.at[k]).wait()
    for i in range(lines):
        back = jnp.dot(circ[...], line_w[i], precision=HIGHEST, preferred_element_type=F32)
        filt[i] = back / line_d[i]
    filt_copy = pltpu.make_async_copy(filt, filt_h, store_sem.at[1])
    filt_copy.start()

    for k in range(2):
        pltpu.make_async_copy(others[k], others[k], line_send.at[k]).wait()
    for k, (n, slots) in enumerate(((ny, slots_y), (nz, slots_z))):
        whole = slots.at[pl.ds(0, n - 1)]
        pltpu.make_async_copy(whole, whole, sum_send.at[k]).wait()
    for step, down, copy in mod_copies:
        @pl.when(there(step))
        def _(copy=copy):
            copy.wait_send()
    wait_sent(1, v1, every)
    wait_sent(2, v2, LOWERS)
    disp_copy.wait()
    filt_copy.wait()


def solution(mesh):
    ny, nz = mesh.shape["gy"], mesh.shape["gz"]
    lines = 32 // nz
    length = 8 * nz
    phases = np.outer(np.arange(length), np.arange(length)) % length
    cosine = np.cos(2.0 * np.pi / length * phases).astype(np.float32)
    sine = np.sin(2.0 * np.pi / length * phases).astype(np.float32)

    def local(force, density, solid_blocks, fixed_nodes, filter_gain):
        vmem = lambda *shape: pltpu.VMEM(shape, F32)
        dma = lambda *shape: pltpu.SemaphoreType.DMA(shape)
        node = [vmem(3, FAR, 128)]
        return pl.pallas_call(
            functools.partial(kernel, ny, nz, lines),
            out_shape=(
                jax.ShapeDtypeStruct((3, 32, 8, 128), F32),
                jax.ShapeDtypeStruct((lines, length, 128), F32),
            ),
            in_specs=[pl.BlockSpec(memory_space=pl.ANY)] * 7,
            out_specs=(pl.BlockSpec(memory_space=pl.ANY),) * 2,
            scratch_shapes=[
                vmem(3, 32, 8, 128), vmem(32, 8, 128), pltpu.VMEM((4, 1, 16), jnp.int32), pltpu.VMEM((32, 8, 128), jnp.int32),
                vmem(1, length), vmem(length, length), vmem(length, length),
                vmem(264, 128), vmem(48, 128), vmem(32, 128), vmem(32, 128), vmem(8, 128),
                vmem(32, 8, 128), vmem(3, 32, 8, 128), vmem(3, 32, 8, 128), vmem(3, 32, 8, 128),
                *(node * 4), vmem(3, 48, 128), vmem(3, 48, 128),
                vmem(3, 32, 8, 128), vmem(3, 32, 8, 128), vmem(3, 512, 128), vmem(3, 512, 128),
                vmem(3, 48, 128), vmem(3, 48, 128), vmem(3, 48, 128), vmem(3, 48, 128),
                vmem(3, 2, 3, 32, 128), vmem(3, 4, 8, 128), vmem(3, 2, 3, 8, 128), vmem(3, 2, 3, 32, 128), vmem(3, 4, 8, 128),
                vmem(512, 128), vmem(32, 8, 128), vmem(16, 128), vmem(ny, 1, 128), vmem(nz, 1, 128),
                vmem(length, length), vmem(32, 8, 128), vmem(lines, length, 128), vmem(lines, length, 128),
                vmem(3, 32, 8, 128), vmem(lines, length, 128),
                dma(7), dma(2), dma(3), dma(3), dma(3, 8), dma(3, 8), dma(2), dma(2), dma(2), dma(2),
            ],
            compiler_params=pltpu.CompilerParams(collective_id=0, has_side_effects=True, vmem_limit_bytes=40 * 1024 * 1024),
            cost_estimate=pl.CostEstimate(flops=60_000_000, bytes_accessed=2_000_000, transcendentals=0),
        )(force, density, solid_blocks, fixed_nodes, filter_gain[None, :], jnp.asarray(cosine), jnp.asarray(sine))

    in_specs = (P(None, "gy", "gz", None), P("gy", "gz", None), P("gy", "gz", None), P("gy", "gz", None), P())
    out_specs = (P(None, "gy", "gz", None), P(("gy", "gz"), None, None))
    return jax.shard_map(local, mesh=mesh, in_specs=in_specs, out_specs=out_specs, check_vma=False)
```

```python
import functools

import jax
import jax.numpy as jnp
import numpy as np
from jax import lax
from jax.experimental import pallas as pl
from jax.experimental.pallas import tpu as pltpu
from jax.sharding import PartitionSpec as P

MIN_MODULUS = 0.1
DIAG_FLOOR = 0.5
POISSON = 0.3
SHEAR = 1.0 / (2.0 * (1.0 + POISSON))
LAME = POISSON / ((1.0 + POISSON) * (1.0 - 2.0 * POISSON))
UNIT = SHEAR / 16.0
VOLUME = 0.5 * LAME / SHEAR
BEND = LAME / (3.0 * SHEAR)
TWIST = 1.0 / 3.0
WARP = (LAME + 4.0 * SHEAR) / 9.0 / SHEAR
KE_DIAG = (LAME + 4.0 * SHEAR) / 9.0
SHIFT = 1.0
PLANE = 16
FAR = 656
F32 = jnp.float32
HIGHEST = lax.Precision.HIGHEST
STEPS = [(-1, 0), (1, 0), (0, -1), (0, 1), (-1, -1), (-1, 1), (1, -1), (1, 1)]
LOWERS = (0, 2, 4)


def stress(y, z, x, m):
    m2, m3, m4 = 2.0 * m, TWIST * m, WARP * m
    gy, gz, gx = {}, {}, {}
    bulk = VOLUME * (y["100"] + z["010"] + x["001"])
    gy["100"] = m2 * (y["100"] + bulk)
    gz["010"] = m2 * (z["010"] + bulk)
    gx["001"] = m2 * (x["001"] + bulk)
    gy["010"] = gz["100"] = m * (y["010"] + z["100"])
    gz["001"] = gx["010"] = m * (z["001"] + x["010"])
    gy["001"] = gx["100"] = m * (y["001"] + x["100"])
    bend = BEND * (z["110"] + x["101"])
    gz["110"], gx["101"] = m * (z["110"] + bend), m * (x["101"] + bend)
    bend = BEND * (y["110"] + x["011"])
    gy["110"], gx["011"] = m * (y["110"] + bend), m * (x["011"] + bend)
    bend = BEND * (y["101"] + z["011"])
    gy["101"], gz["011"] = m * (y["101"] + bend), m * (z["011"] + bend)
    twist = y["011"] + z["101"] + x["110"]
    gy["011"] = m3 * (y["011"] + twist)
    gz["101"] = m3 * (z["101"] + twist)
    gx["110"] = m3 * (x["110"] + twist)
    gy["111"], gz["111"], gx["111"] = m4 * y["111"], m4 * z["111"], m4 * x["111"]
    return gy, gz, gx


FORMS = ((0, 0), (0, 1), (1, 1), (2, 0), (2, 1), (2, 2))


def dot_forms(coefs, pulled):
    total = None
    for c, g in zip(coefs, pulled):
        for key in g:
            term = c[key] * g[key]
            total = term if total is None else total + term
    return total


def pair_y(low, high):
    coefs = []
    for a, b in zip(low, high):
        c = {}
        for key in a:
            if key != "00":
                c["0" + key] = a[key] + b[key]
            c["1" + key] = b[key] - a[key]
        coefs.append(c)
    return coefs


def spread_y(g):
    low, high = {}, {}
    for key in ("00", "01", "10", "11"):
        d = g["1" + key]
        if key == "00":
            low[key], high[key] = -d, d
        else:
            s = g["0" + key]
            low[key], high[key] = s - d, s + d
    return low, high


def kernel(
    ny, nz, lines,
    force_h, dens_h, solid_h, fixed_h, gain_h, cos_h, sin_h,
    disp_h, filt_h,
    force, dens, solid, fixed, gain, cosine, sine,
    mod, mod_z, sum_low, sum_high, high_z,
    inv, r0, w0, w1, v0, v1, v2, x0, x1, x2, low_z, low_zx,
    a_low, b_low, a_up, b_up, p_low, p_up, q_low, q_up,
    first_y, first_z, first_c, seen_y, seen_z, seen_c,
    stage_z, stage_c, land_y, land_z, land_c,
    tmp, sums, acc, slots_y, slots_z, forms,
    circ, weighted, line_w, line_d, disp, filt,
    load_sem, store_sem, first_send, first_recv, halo_send, halo_recv, sum_send, sum_recv, line_send, line_recv,
):
    iy, iz = lax.axis_index("gy"), lax.axis_index("gz")
    lane = lax.broadcasted_iota(jnp.int32, (8, 128), 1)
    first_lane, last_lane = lane == 0, lane == 127
    zeros = jnp.zeros((8, 128), F32)

    def at_upper(u):
        return jnp.where(last_lane, 0.0, pltpu.roll(u, 127, 1))

    def from_lower(u):
        return jnp.where(first_lane, 0.0, pltpu.roll(u, 1, 1))

    def modulus(e):
        return mod[pl.ds(8 * e if isinstance(e, int) else pl.multiple_of(8 * e, 8), 8), :]

    loads = [
        pltpu.make_async_copy(src, dst, load_sem.at[i])
        for i, (src, dst) in enumerate(
            [(dens_h, dens), (solid_h, solid), (fixed_h, fixed), (force_h, force), (gain_h, gain), (cos_h, cosine), (sin_h, sine)]
        )
    ]
    for load in loads:
        load.start()

    barrier = pltpu.get_barrier_semaphore()

    def ring(sy, sz):
        return {"gy": lax.rem(iy + sy + ny, ny), "gz": lax.rem(iz + sz + nz, nz)}

    for sy, sz in STEPS:
        pl.semaphore_signal(barrier, 1, device_id=ring(sy, sz))

    def greet_z(i, carry):
        pl.semaphore_signal(barrier, 1, device_id={"gz": lax.rem(iz + i, nz)})
        return carry

    def greet_y(i, carry):
        pl.semaphore_signal(barrier, 1, device_id={"gy": lax.rem(iy + i, ny)})
        return carry

    lax.fori_loop(2, nz - 1, greet_z, 0)
    lax.fori_loop(2, ny - 1, greet_y, 0)

    def there(step):
        sy, sz = step
        ok = None
        for index, s, n in ((iy, sy, ny), (iz, sz, nz)):
            if s:
                here = index >= 1 if s < 0 else index < n - 1
                ok = here if ok is None else jnp.logical_and(ok, here)
        return ok

    def device(step):
        return {"gy": iy + step[0], "gz": iz + step[1]}

    loads[0].wait()
    loads[1].wait()
    flags = solid[:, 0, :].astype(F32)
    spread = (
        lax.broadcasted_iota(jnp.int32, (16, 128), 1) // 8 == lax.broadcasted_iota(jnp.int32, (16, 128), 0)
    ).astype(F32)
    solid_rows = jnp.dot(flags, spread, precision=HIGHEST, preferred_element_type=F32)
    for block in range(4):
        row = solid_rows[block : block + 1]
        for y in range(8 * block, 8 * block + 8):
            d = dens[y]
            mod[pl.ds(8 * (y + 1), 8), :] = row * (UNIT * MIN_MODULUS + (UNIT * (1.0 - MIN_MODULUS)) * (d * d * d))

    loads[2].wait()
    loads[3].wait()
    for c in range(3):
        def body(i, carry, c=c):
            for k in range(4):
                y = 4 * i + k
                r0[pl.ds(pl.multiple_of(256 * c + 8 * y, 8), 8), :] = jnp.where(fixed[y] != 0, 0.0, force[c, y])
            return carry
        lax.fori_loop(0, 8, body, 0)

    for side, y, moduli in ((0, 0, (0,)), (1, 31, (30, 31))):
        for c in range(3):
            first_y[side, c] = r0[pl.ds(256 * c + 8 * y, 8), :]
        for k, e in enumerate(moduli):
            first_y[side, 3 + k] = modulus(e + 1)
    for side, z, moduli in ((0, 0, (0,)), (1, 7, (6, 7))):
        for j in range(4):
            rows = pl.ds(8 * j, 8)
            for c in range(3):
                first_z[side, c, rows, :] = r0[pl.ds(256 * c + 64 * j + z, 8, 8), :]
            for k, e in enumerate(moduli):
                first_z[side, 3 + k, rows, :] = mod[pl.ds(64 * j + 8 + e, 8, 8), :]
    for i, (sy, sz) in enumerate(STEPS[4:]):
        for c in range(3):
            first_c[i, pl.ds(c, 1), :] = r0[pl.ds(256 * c + 8 * (0 if sy < 0 else 31) + (0 if sz < 0 else 7), 1), :]
        spots = [(y, z) for y in ((0,) if sy < 0 else (30, 31)) for z in ((0,) if sz < 0 else (6, 7))]
        for k, (y, z) in enumerate(spots):
            first_c[i, pl.ds(3 + k, 1), :] = mod[pl.ds(8 * (y + 1) + z, 1), :]

    pl.semaphore_wait(barrier, 8 + max(nz - 3, 0) + max(ny - 3, 0))

    def part_of(arrays, i):
        return arrays[0].at[i] if i < 2 else arrays[1].at[i - 2] if i < 4 else arrays[2].at[i - 4]

    seen = (seen_y, seen_z, seen_c)
    first_copies = [
        pltpu.make_async_remote_copy(
            part_of((first_y, first_z, first_c), i), part_of(seen, i), first_send.at[i], first_recv.at[i],
            device_id=device(step))
        for i, step in enumerate(STEPS)
    ]
    ORDER = (7, 6, 5, 4, 2, 3, 0, 1)
    for i in ORDER:
        @pl.when(there(STEPS[i]))
        def _(i=i):
            first_copies[i].start()

    def away(i):
        return jnp.logical_not(there((-STEPS[i][0], -STEPS[i][1])))

    for i in range(8):
        @pl.when(away(i))
        def _(i=i):
            ref = part_of(seen, i)
            ref[...] = jnp.zeros(ref.shape, F32)

    rows_x = max(nz // 8, 1)
    cols_z = nz // rows_x

    def hops(i):
        dx, dz = i // cols_z, i % cols_z
        return -(min(dx, rows_x - dx) + min(dz, cols_z - dz))

    def other_z(i):
        x = lax.rem(iz // cols_z + i // cols_z, rows_x)
        return x * cols_z + lax.rem(iz + i % cols_z, cols_z)

    far_first = sorted(range(1, nz), key=hops)
    mine = pl.ds(pl.multiple_of(iz * 8, 8), 8)
    for i in far_first:
        to = other_z(i)
        pltpu.make_async_remote_copy(
            dens.at[pl.ds(to * lines, lines)], line_d.at[:, mine, :],
            line_send.at[0], line_recv.at[0], device_id={"gz": to},
        ).start()
    for i in range(lines):
        line_d[i, mine, :] = dens[iz * lines + i]

    for load in loads[4:]:
        load.wait()
    length = cosine.shape[0]
    gains = gain[...] * (1.0 / length)
    circ[...] = jnp.dot(cosine[...] * gains, cosine[...], precision=HIGHEST, preferred_element_type=F32) + jnp.dot(
        sine[...] * gains, sine[...], precision=HIGHEST, preferred_element_type=F32)

    def halo_copies(k, src, which):
        copies = []
        for i in which:
            sy, sz = STEPS[i]
            if sz == 0:
                s, d = src.at[:, pl.ds(PLANE * (1 if sy < 0 else 32), 8), :], land_y.at[k, i]
            elif sy == 0:
                s, d = stage_z.at[k, i - 2], land_z.at[k, i - 2]
            else:
                s, d = stage_c.at[k, i - 4], land_c.at[k, i - 4]
            copies.append((i, pltpu.make_async_remote_copy(
                s, d, halo_send.at[k, i], halo_recv.at[k, i], device_id=device(STEPS[i]))))
        return copies

    def send_halo(k, src, which):
        for c in range(3):
            for side, z in ((0, 0), (1, 7)):
                if side + 2 in which:
                    for j in range(4):
                        stage_z[k, side, c, pl.ds(8 * j, 8), :] = src[c, pl.ds(PLANE * (8 * j + 1) + z, 8, PLANE), :]
            for i in which:
                if i >= 4:
                    row = PLANE * (1 if STEPS[i][0] < 0 else 32) + (0 if STEPS[i][1] < 0 else 7)
                    stage_c[k, i - 4, pl.ds(c, 1), :] = src[c, pl.ds(row, 1), :]
        for i, copy in sorted(halo_copies(k, src, which), key=lambda item: ORDER.index(item[0])):
            @pl.when(there(STEPS[i]))
            def _(copy=copy):
                copy.start()

    def land_of(k, i):
        return land_y.at[k, i] if i < 2 else land_z.at[k, i - 2] if i < 4 else land_c.at[k, i - 4]

    def clear_halo(k, which):
        for i in which:
            @pl.when(jnp.logical_not(there((-STEPS[i][0], -STEPS[i][1]))))
            def _(i=i):
                ref = land_of(k, i)
                ref[...] = jnp.zeros(ref.shape, F32)

    def wait_halo(k, src, which):
        for i, copy in halo_copies(k, src, which):
            @pl.when(there((-STEPS[i][0], -STEPS[i][1])))
            def _(copy=copy):
                copy.wait_recv()

    def wait_sent(k, src, which):
        for i, copy in halo_copies(k, src, which):
            @pl.when(there(STEPS[i]))
            def _(copy=copy):
                copy.wait_send()

    def put(ref, vx, rows, u):
        ref[rows] = u
        vx[rows] = at_upper(u)

    def place_halo(k, ref, vx, which):
        for c in range(3):
            put(ref, vx, (c, pl.ds(PLANE * 33, 8), slice(None)), land_y[k, 0, c])
            if 1 in which:
                put(ref, vx, (c, pl.ds(0, 8), slice(None)), land_y[k, 1, c])
            for j in range(4):
                rows = (c, pl.ds(PLANE * (8 * j + 1) + 8, 8, PLANE), slice(None))
                put(ref, vx, rows, land_z[k, 0, c, pl.ds(8 * j, 8), :])
                if 3 in which:
                    u = land_z[k, 1, c, pl.ds(8 * j, 8), :]
                    low_z[c, pl.ds(8 * j + 1, 8), :] = u
                    low_zx[c, pl.ds(8 * j + 1, 8), :] = at_upper(u)
        for i in which:
            if i < 4:
                continue
            u = land_c[k, i - 4]
            ux = at_upper(u)
            y_row = 33 if STEPS[i][0] < 0 else 0
            for c in range(3):
                if STEPS[i][1] < 0:
                    ref[c, pl.ds(PLANE * y_row + 8, 1), :] = u[c : c + 1]
                    vx[c, pl.ds(PLANE * y_row + 8, 1), :] = ux[c : c + 1]
                else:
                    low_z[c, pl.ds(y_row, 1), :] = u[c : c + 1]
                    low_zx[c, pl.ds(y_row, 1), :] = ux[c : c + 1]

    def pair_zx(u0, x0, u1, x1):
        s0, d0, s1, d1 = u0 + x0, x0 - u0, u1 + x1, x1 - u1
        return {"00": s0 + s1, "01": d0 + d1, "10": s1 - s0, "11": d1 - d0}

    def plane(ref, vx, row):
        row = pl.multiple_of(row, PLANE)
        return [
            pair_zx(ref[c, pl.ds(row, 8), :], vx[c, pl.ds(row, 8), :], ref[c, pl.ds(row + 1, 8), :], vx[c, pl.ds(row + 1, 8), :])
            for c in range(3)
        ]

    def low_layer(ref, vx):
        for j in range(5):
            def rows(start):
                return [
                    pair_zx(
                        low_z[c, pl.ds(start, 8), :], low_zx[c, pl.ds(start, 8), :],
                        ref[c, pl.ds(PLANE * start, 8, PLANE), :], vx[c, pl.ds(PLANE * start, 8, PLANE), :])
                    for c in range(3)
                ]
            coefs = pair_y(rows(8 * j), rows(8 * j + 1))
            for c, g in enumerate(stress(*coefs, mod_z[pl.ds(8 * j + 1, 8), :])):
                for part, start, pa, pb in zip(spread_y(g), (8 * j, 8 * j + 1), (p_low, p_up), (q_low, q_up)):
                    s, d = part["00"] + part["10"], part["01"] + part["11"]
                    pa[c, pl.ds(start, 8), :] = s - d
                    pb[c, pl.ds(start, 8), :] = s + d
        for c in range(3):
            for j in range(4):
                rows = pl.ds(8 * j + 1, 8)
                to = (c, pl.ds(PLANE * 8 * j, 8, PLANE), slice(None))
                a_up[to] = p_low[c, rows, :] + p_up[c, rows, :]
                b_up[to] = q_low[c, rows, :] + q_up[c, rows, :]

    def flat(planes):
        return tuple(p[key] for p in planes for key in ("00", "01", "10", "11"))

    def unflat(values):
        keys = ("00", "01", "10", "11")
        return [dict(zip(keys, values[4 * c : 4 * c + 4])) for c in range(3)]

    def forces(ref, vx):
        low, high = plane(ref, vx, 0), plane(ref, vx, PLANE)
        upper = [spread_y(g)[1] for g in stress(*pair_y(low, high), modulus(0))]

        def one(e, low, upper):
            high = plane(ref, vx, PLANE * (e + 1))
            new = []
            for c, g in enumerate(stress(*pair_y(low, high), modulus(e))):
                lo, hi = spread_y(g)
                t = {key: upper[c][key] + lo[key] for key in lo}
                new.append(hi)
                sa, sb, da, db = t["00"] - t["01"], t["00"] + t["01"], t["10"] - t["11"], t["10"] + t["11"]
                row = pl.multiple_of(PLANE * (e - 1), PLANE)
                a_low[c, e - 1] = sa - da
                b_low[c, e - 1] = sb - db
                a_up[c, pl.ds(row + 1, 8), :] = sa + da
                b_up[c, pl.ds(row + 1, 8), :] = sb + db
            return high, new

        def body(i, carry):
            low, upper = unflat(carry[:12]), unflat(carry[12:])
            for k in range(4):
                low, upper = one(4 * i + 1 + k, low, upper)
            return flat(low) + flat(upper)

        lax.fori_loop(0, 8, body, flat(high) + flat(upper))

    def finish(ref, image, after, after_x):
        def body(i, carry):
            for k in range(4):
                y = 4 * i + k
                held = fixed[y] != 0
                scale = inv[y]
                row = pl.multiple_of(PLANE * y, PLANE)
                for c in range(3):
                    f = (a_low[c, y] + a_up[c, pl.ds(row, 8), :]) + from_lower(b_low[c, y] + b_up[c, pl.ds(row, 8), :])
                    v = ref[c, pl.ds(row + PLANE, 8), :]
                    w = jnp.where(held, v, f)
                    image[c, y] = w
                    new = scale * w - SHIFT * v
                    after[c, pl.ds(row + PLANE, 8), :] = new
                    after_x[c, pl.ds(row + PLANE, 8), :] = at_upper(new)
            return carry
        lax.fori_loop(0, 8, body, 0)

    def dots(pairs):
        def get(ref, c, y):
            if ref.shape[0] == 768:
                return ref[pl.ds(pl.multiple_of(256 * c + 8 * y, 8), 8), :]
            if ref.shape[1] == FAR:
                return ref[c, pl.ds(pl.multiple_of(PLANE * y + PLANE, PLANE), 8), :]
            return ref[c, y]

        def body(i, carry):
            carry = list(carry)
            for k in range(2):
                for c in range(3):
                    held = {}
                    for p, (slot, a, b) in enumerate(pairs):
                        for ref in (a, b):
                            if id(ref) not in held:
                                held[id(ref)] = get(ref, c, 2 * i + k)
                        carry[p] = carry[p] + held[id(a)] * held[id(b)]
            return tuple(carry)

        total = lax.fori_loop(0, 16, body, (zeros,) * len(pairs))
        for (slot, a, b), t in zip(pairs, total):
            acc[pl.ds(slot, 1), :] = jnp.sum(t, axis=0, keepdims=True)

    every = tuple(range(8))
    clear_halo(0, every)
    clear_halo(1, LOWERS)
    acc[...] = jnp.zeros(acc.shape, F32)

    for i in range(8):
        @pl.when(jnp.logical_not(away(i)))
        def _(i=i):
            first_copies[i].wait_recv()

    mod[pl.ds(0, 8), :] = seen_y[1, 4]

    def row_of(u, k):
        return u[k : k + 1]

    low_low, up_low, low_up, up_up = seen_c[3], seen_c[1], seen_c[2], seen_c[0]
    for row, z1, z2, z7, z8 in (
        (0, row_of(low_low, 4), row_of(low_low, 3), row_of(seen_y[1, 3], 7), row_of(low_up, 3)),
        (1, row_of(low_low, 6), row_of(low_low, 5), row_of(seen_y[1, 4], 7), row_of(low_up, 4)),
        (34, row_of(up_low, 4), row_of(up_low, 3), row_of(seen_y[0, 3], 7), row_of(up_up, 3)),
    ):
        at = pl.ds(row, 1)
        mod_z[at, :] = z1
        sum_low[at, :] = z1 + z2
        sum_high[at, :] = z7 + z8
    for j in range(4):
        rows, to = pl.ds(8 * j, 8), pl.ds(8 * j + 2, 8)
        z1 = seen_z[1, 4, rows, :]
        mod_z[to, :] = z1
        sum_low[to, :] = z1 + seen_z[1, 3, rows, :]
        sum_high[to, :] = first_z[1, 4, rows, :] + seen_z[0, 3, rows, :]
    for c in range(3):
        for row, low, high in ((0, low_low, low_up), (33, up_low, up_up)):
            low_z[c, pl.ds(row, 1), :] = row_of(low, c)
            high_z[c, pl.ds(row, 1), :] = row_of(high, c)
        for j in range(4):
            rows, to = pl.ds(8 * j, 8), pl.ds(8 * j + 1, 8)
            low_z[c, to, :] = seen_z[1, c, rows, :]
            high_z[c, to, :] = seen_z[0, c, rows, :]

    def inverse_of(t):
        return 1.0 / jnp.maximum((KE_DIAG / UNIT) * (t + from_lower(t)), DIAG_FLOOR)

    for j in range(5):
        rows, above = pl.ds(8 * j, 8), pl.ds(8 * j + 1, 8)
        low_scale = inverse_of(sum_low[rows, :] + sum_low[above, :])
        high_scale = inverse_of(sum_high[rows, :] + sum_high[above, :])
        tmp[pl.ds(PLANE * 8 * j, 8, PLANE), :] = mod_z[rows, :] + mod_z[above, :]
        for c in range(3):
            u = low_scale * low_z[c, rows, :]
            low_z[c, rows, :] = u
            low_zx[c, rows, :] = at_upper(u)
            put(v0, x0, (c, pl.ds(PLANE * 8 * j + 8, 8, PLANE), slice(None)), high_scale * high_z[c, rows, :])

    def keep_sum(n, t):
        row = PLANE * n if isinstance(n, int) else pl.multiple_of(PLANE * n, PLANE)
        sums[n] = t
        tmp[pl.ds(row + 1, 8), :] = t

    def begin(n, loads_of):
        row = PLANE * n if isinstance(n, int) else pl.multiple_of(PLANE * n, PLANE)
        scale = inverse_of(sums[n] + tmp[pl.ds(row, 8), :])
        for c in range(3):
            put(v0, x0, (c, pl.ds(row, 8), slice(None)), scale * loads_of(c))
        return scale

    keep_sum(0, seen_y[1, 3] + seen_y[1, 4])
    keep_sum(33, modulus(32) + seen_y[0, 3])

    def sum_own(i, carry):
        for k in range(4):
            y = 4 * i + k
            keep_sum(y + 1, modulus(y) + modulus(y + 1))
        return carry
    lax.fori_loop(0, 8, sum_own, 0)
    begin(0, lambda c: seen_y[1, c])
    begin(33, lambda c: seen_y[0, c])

    def begin_own(i, carry):
        for k in range(4):
            y = 4 * i + k
            inv[y] = begin(y + 1, lambda c: r0[pl.ds(pl.multiple_of(256 * c + 8 * y, 8), 8), :])
        return carry
    lax.fori_loop(0, 8, begin_own, 0)

    low_layer(v0, x0)
    forces(v0, x0)
    finish(v0, w0, v1, x1)
    send_halo(0, v1, every)
    dots([(0, r0, v0), (1, r0, v1), (3, v0, w0), (4, v1, w0)])
    wait_halo(0, v1, every)
    place_halo(0, v1, x1, every)
    low_layer(v1, x1)
    forces(v1, x1)
    finish(v1, w1, v2, x2)
    send_halo(1, v2, LOWERS)
    dots([(2, r0, v2), (5, v2, w0), (6, v1, w1), (7, v2, w1)])
    solid_scale = (-3.0 * (1.0 - MIN_MODULUS) * UNIT) * solid_rows
    for block in range(4):
        row = solid_scale[block : block + 1]
        for y in range(8 * block, 8 * block + 8):
            d = dens[y]
            weighted[y] = row * (d * d * d)
    wait_halo(1, v2, LOWERS)
    place_halo(1, v2, x2, LOWERS)

    basis = ((v0, x0), (v1, x1), (v2, x2))

    def element_forms(chosen, pairs, with_total):
        def body(i, carry):
            lows = [unflat(carry[12 * k : 12 * k + 12]) for k in range(len(chosen))]
            for k in range(2):
                y = 2 * i + k
                highs = [plane(*basis[b], PLANE * (y + 2)) for b in chosen]
                coefs = {b: pair_y(low, high) for b, low, high in zip(chosen, lows, highs)}
                factor = weighted[y]
                for a in sorted({a for a, _ in pairs}):
                    pulled = stress(*coefs[a], 1.0)
                    for slot, (p, q) in enumerate(FORMS):
                        if (p, q) in pairs and p == a:
                            e = dot_forms(coefs[q], pulled)
                            forms[slot, y] = factor * e
                            if with_total:
                                carry = carry[:-1] + (carry[-1] + modulus(y + 1) * e,)
                lows = highs
            out = ()
            for low in lows:
                out = out + flat(low)
            return out + (carry[12 * len(chosen) :] if with_total else ())
        init = ()
        for b in chosen:
            init = init + flat(plane(*basis[b], PLANE))
        return lax.fori_loop(0, 16, body, init + ((zeros,) if with_total else ()))

    total = element_forms((2,), ((2, 2),), True)[-1]
    acc[pl.ds(8, 1), :] = jnp.sum(total, axis=0, keepdims=True)

    column = jnp.sum(acc[...], axis=1, keepdims=True)
    rows = lax.broadcasted_iota(jnp.int32, (16, 128), 0)
    lanes = lax.broadcasted_iota(jnp.int32, (16, 128), 1)
    part = jnp.sum(jnp.where(rows == lanes, column, 0.0), axis=0, keepdims=True)
    for k, (axis, me, n, slots) in enumerate((("gy", iy, ny, slots_y), ("gz", iz, nz, slots_z))):
        slots[me] = part

        far_y = sorted(range(1, ny), key=lambda i: -min(i, ny - i))
        for i in far_y if axis == "gy" else far_first:
            pltpu.make_async_remote_copy(
                slots.at[me], slots.at[me], sum_send.at[k], sum_recv.at[k],
                device_id={axis: lax.rem(me + i, n) if axis == "gy" else other_z(i)},
            ).start()
        if k == 0:
            element_forms((0, 1), ((0, 0), (0, 1), (1, 1)), False)
        else:
            element_forms((0, 1, 2), ((2, 0), (2, 1)), False)
        whole = slots.at[pl.ds(0, n - 1)]
        pltpu.make_async_copy(whole, whole, sum_recv.at[k]).wait()
        part = jnp.sum(slots[:, 0, :], axis=0, keepdims=True)

    lane1 = lax.broadcasted_iota(jnp.int32, (1, 128), 1)

    def entry(i):
        return jnp.sum(jnp.where(lane1 == i, part, 0.0), axis=1, keepdims=True)

    b0, b1, b2, g00, g10, g20, g11, g21, g22 = (entry(i) for i in range(9))
    l10, l20 = g10 / g00, g20 / g00
    d1 = g11 - l10 * g10
    e21 = g21 - l20 * g10
    l21 = e21 / d1
    d2 = g22 - l20 * g20 - l21 * e21
    y1 = b1 - l10 * b0
    y2 = b2 - l20 * b0 - l21 * y1
    c2 = y2 / d2
    c1 = y1 / d1 - l21 * c2
    c0 = b0 / g00 - l10 * c1 - l20 * c2
    wide = lambda c: jnp.broadcast_to(c, (8, 128))
    factors = [wide(c) for c in (c0 * c0, 2.0 * c0 * c1, c1 * c1, 2.0 * c2 * c0, 2.0 * c2 * c1, c2 * c2)]
    c0, c1, c2 = wide(c0), wide(c1), wide(c2)

    def weigh(i, carry):
        for k in range(4):
            y = 4 * i + k
            total = factors[0] * forms[0, y]
            for slot in range(1, 6):
                total = total + factors[slot] * forms[slot, y]
            weighted[y] = total
        return carry
    lax.fori_loop(0, 8, weigh, 0)

    for i in far_first:
        to = other_z(i)
        pltpu.make_async_remote_copy(
            weighted.at[pl.ds(to * lines, lines)], line_w.at[:, mine, :],
            line_send.at[1], line_recv.at[1], device_id={"gz": to},
        ).start()
    for i in range(lines):
        line_w[i, mine, :] = weighted[iz * lines + i]

    def displace(i, carry):
        for k in range(4):
            row = pl.multiple_of(PLANE * (4 * i + k + 1), PLANE)
            for c in range(3):
                rows = (c, pl.ds(row, 8), slice(None))
                disp[c, 4 * i + k] = c0 * v0[rows] + c1 * v1[rows] + c2 * v2[rows]
        return carry
    lax.fori_loop(0, 8, displace, 0)
    disp_copy = pltpu.make_async_copy(disp, disp_h, store_sem.at[0])
    disp_copy.start()

    others = [ref.at[:, pl.ds(0, 8 * (nz - 1)), :] for ref in (line_d, line_w)]
    for k in range(2):
        pltpu.make_async_copy(others[k], others[k], line_recv.at[k]).wait()
    for i in range(lines):
        back = jnp.dot(circ[...], line_w[i], precision=HIGHEST, preferred_element_type=F32)
        filt[i] = back / line_d[i]
    filt_copy = pltpu.make_async_copy(filt, filt_h, store_sem.at[1])
    filt_copy.start()

    for k in range(2):
        pltpu.make_async_copy(others[k], others[k], line_send.at[k]).wait()
    for k, (n, slots) in enumerate(((ny, slots_y), (nz, slots_z))):
        whole = slots.at[pl.ds(0, n - 1)]
        pltpu.make_async_copy(whole, whole, sum_send.at[k]).wait()
    for i in range(8):
        @pl.when(there(STEPS[i]))
        def _(i=i):
            first_copies[i].wait_send()
    wait_sent(0, v1, every)
    wait_sent(1, v2, LOWERS)
    disp_copy.wait()
    filt_copy.wait()


def solution(mesh):
    ny, nz = mesh.shape["gy"], mesh.shape["gz"]
    lines = 32 // nz
    length = 8 * nz
    phases = np.outer(np.arange(length), np.arange(length)) % length
    cosine = np.cos(2.0 * np.pi / length * phases).astype(np.float32)
    sine = np.sin(2.0 * np.pi / length * phases).astype(np.float32)

    def local(force, density, solid_blocks, fixed_nodes, filter_gain):
        vmem = lambda *shape: pltpu.VMEM(shape, F32)
        dma = lambda *shape: pltpu.SemaphoreType.DMA(shape)
        node = [vmem(3, FAR, 128)]
        return pl.pallas_call(
            functools.partial(kernel, ny, nz, lines),
            out_shape=(
                jax.ShapeDtypeStruct((3, 32, 8, 128), F32),
                jax.ShapeDtypeStruct((lines, length, 128), F32),
            ),
            in_specs=[pl.BlockSpec(memory_space=pltpu.HBM)] * 7,
            out_specs=(pl.BlockSpec(memory_space=pltpu.HBM),) * 2,
            scratch_shapes=[
                vmem(3, 32, 8, 128), vmem(32, 8, 128), pltpu.VMEM((4, 1, 16), jnp.int32), pltpu.VMEM((32, 8, 128), jnp.int32),
                vmem(1, length), vmem(length, length), vmem(length, length),
                vmem(264, 128), vmem(48, 128), vmem(48, 128), vmem(48, 128), vmem(3, 48, 128),
                vmem(32, 8, 128), vmem(768, 128), vmem(3, 32, 8, 128), vmem(3, 32, 8, 128),
                *(node * 6), vmem(3, 48, 128), vmem(3, 48, 128),
                vmem(3, 32, 8, 128), vmem(3, 32, 8, 128), vmem(3, 640, 128), vmem(3, 640, 128),
                vmem(3, 48, 128), vmem(3, 48, 128), vmem(3, 48, 128), vmem(3, 48, 128),
                vmem(2, 5, 8, 128), vmem(2, 5, 32, 128), vmem(4, 8, 128),
                vmem(2, 5, 8, 128), vmem(2, 5, 32, 128), vmem(4, 8, 128),
                vmem(2, 2, 3, 32, 128), vmem(2, 4, 8, 128), vmem(2, 2, 3, 8, 128), vmem(2, 2, 3, 32, 128), vmem(2, 4, 8, 128),
                vmem(FAR, 128), vmem(34, 8, 128), vmem(16, 128), vmem(ny, 1, 128), vmem(nz, 1, 128), vmem(6, 32, 8, 128),
                vmem(length, length), vmem(32, 8, 128), vmem(lines, length, 128), vmem(lines, length, 128),
                vmem(3, 32, 8, 128), vmem(lines, length, 128),
                dma(7), dma(2), dma(8), dma(8), dma(2, 8), dma(2, 8), dma(2), dma(2), dma(2), dma(2),
            ],
            compiler_params=pltpu.CompilerParams(collective_id=0, has_side_effects=True, vmem_limit_bytes=62 * 1024 * 1024),
            cost_estimate=pl.CostEstimate(flops=60_000_000, bytes_accessed=2_000_000, transcendentals=0),
        )(force, density, solid_blocks, fixed_nodes, filter_gain[None, :], jnp.asarray(cosine), jnp.asarray(sine))

    in_specs = (P(None, "gy", "gz", None), P("gy", "gz", None), P("gy", "gz", None), P("gy", "gz", None), P())
    out_specs = (P(None, "gy", "gz", None), P(("gy", "gz"), None, None))
    return jax.shard_map(local, mesh=mesh, in_specs=in_specs, out_specs=out_specs, check_vma=False)
```

```python
import functools

import jax
import jax.numpy as jnp
import numpy as np
from jax import lax
from jax.experimental import pallas as pl
from jax.experimental.pallas import tpu as pltpu
from jax.sharding import PartitionSpec as P

MIN_MODULUS = 0.1
DIAG_FLOOR = 0.5
POISSON = 0.3
SHEAR = 1.0 / (2.0 * (1.0 + POISSON))
LAME = POISSON / ((1.0 + POISSON) * (1.0 - 2.0 * POISSON))
UNIT = SHEAR / 16.0
VOLUME = 0.5 * LAME / SHEAR
BEND = LAME / (3.0 * SHEAR)
TWIST = 1.0 / 3.0
WARP = (LAME + 4.0 * SHEAR) / 9.0 / SHEAR
KE_DIAG = (LAME + 4.0 * SHEAR) / 9.0
SHIFT = 1.0
PLANE = 16
FAR = 656
F32 = jnp.float32
HIGHEST = lax.Precision.HIGHEST
STEPS = [(-1, 0), (1, 0), (0, -1), (0, 1), (-1, -1), (-1, 1), (1, -1), (1, 1)]
LOWERS = (0, 2, 4)


def stress(y, z, x, m):
    m2, m3, m4 = 2.0 * m, TWIST * m, WARP * m
    gy, gz, gx = {}, {}, {}
    bulk = VOLUME * (y["100"] + z["010"] + x["001"])
    gy["100"] = m2 * (y["100"] + bulk)
    gz["010"] = m2 * (z["010"] + bulk)
    gx["001"] = m2 * (x["001"] + bulk)
    gy["010"] = gz["100"] = m * (y["010"] + z["100"])
    gz["001"] = gx["010"] = m * (z["001"] + x["010"])
    gy["001"] = gx["100"] = m * (y["001"] + x["100"])
    bend = BEND * (z["110"] + x["101"])
    gz["110"], gx["101"] = m * (z["110"] + bend), m * (x["101"] + bend)
    bend = BEND * (y["110"] + x["011"])
    gy["110"], gx["011"] = m * (y["110"] + bend), m * (x["011"] + bend)
    bend = BEND * (y["101"] + z["011"])
    gy["101"], gz["011"] = m * (y["101"] + bend), m * (z["011"] + bend)
    twist = y["011"] + z["101"] + x["110"]
    gy["011"] = m3 * (y["011"] + twist)
    gz["101"] = m3 * (z["101"] + twist)
    gx["110"] = m3 * (x["110"] + twist)
    gy["111"], gz["111"], gx["111"] = m4 * y["111"], m4 * z["111"], m4 * x["111"]
    return gy, gz, gx


FORMS = ((0, 0), (0, 1), (1, 1), (2, 0), (2, 1), (2, 2))


def dot_forms(coefs, pulled):
    total = None
    for c, g in zip(coefs, pulled):
        for key in g:
            term = c[key] * g[key]
            total = term if total is None else total + term
    return total


def pair_y(low, high):
    coefs = []
    for a, b in zip(low, high):
        c = {}
        for key in a:
            if key != "00":
                c["0" + key] = a[key] + b[key]
            c["1" + key] = b[key] - a[key]
        coefs.append(c)
    return coefs


def spread_y(g):
    low, high = {}, {}
    for key in ("00", "01", "10", "11"):
        d = g["1" + key]
        if key == "00":
            low[key], high[key] = -d, d
        else:
            s = g["0" + key]
            low[key], high[key] = s - d, s + d
    return low, high


def kernel(
    ny, nz, lines,
    force_h, dens_h, solid_h, fixed_h, gain_h, cos_h, sin_h,
    disp_h, filt_h,
    force, dens, solid, fixed, gain, cosine, sine,
    mod, mod_z, sum_low, sum_high, high_z,
    inv, r0, w0, w1, v0, v1, v2, x0, x1, x2, low_z, low_zx,
    a_low, b_low, a_up, b_up, p_low, p_up, q_low, q_up,
    first_y, first_z, first_c, seen_y, seen_z, seen_c,
    stage_z, stage_c, land_y, land_z, land_c,
    tmp, sums, acc, slots_y, slots_z, forms,
    circ, weighted, line_w, line_d, disp, filt,
    load_sem, store_sem, first_send, first_recv, halo_send, halo_recv, sum_send, sum_recv, line_send, line_recv, greet_sem,
):
    iy, iz = lax.axis_index("gy"), lax.axis_index("gz")
    lane = lax.broadcasted_iota(jnp.int32, (8, 128), 1)
    first_lane, last_lane = lane == 0, lane == 127
    zeros = jnp.zeros((8, 128), F32)

    def at_upper(u):
        return jnp.where(last_lane, 0.0, pltpu.roll(u, 127, 1))

    def from_lower(u):
        return jnp.where(first_lane, 0.0, pltpu.roll(u, 1, 1))

    def modulus(e):
        return mod[pl.ds(8 * e if isinstance(e, int) else pl.multiple_of(8 * e, 8), 8), :]

    loads = [
        pltpu.make_async_copy(src, dst, load_sem.at[i])
        for i, (src, dst) in enumerate(
            [(dens_h, dens), (solid_h, solid), (fixed_h, fixed), (force_h, force), (gain_h, gain), (cos_h, cosine), (sin_h, sine)]
        )
    ]
    for load in loads:
        load.start()

    barrier = pltpu.get_barrier_semaphore()

    def ring(sy, sz):
        return {"gy": lax.rem(iy + sy + ny, ny), "gz": lax.rem(iz + sz + nz, nz)}

    for sy, sz in STEPS:
        pl.semaphore_signal(barrier, 1, device_id=ring(sy, sz))

    def greeters(r):
        return [(a, axis, n) for a, (axis, n) in enumerate((("gy", ny), ("gz", nz))) if n >= 4 << r]

    def greet(r):
        for a, axis, n in greeters(r):
            for d in (1 << r, n - (1 << r)):
                to = lax.rem((iy if axis == "gy" else iz) + d, n)
                pl.semaphore_signal(greet_sem.at[a, r], 1, device_id={axis: to})

    def greeted(r):
        for a, axis, n in greeters(r):
            pl.semaphore_wait(greet_sem.at[a, r], 2)

    def there(step):
        sy, sz = step
        ok = None
        for index, s, n in ((iy, sy, ny), (iz, sz, nz)):
            if s:
                here = index >= 1 if s < 0 else index < n - 1
                ok = here if ok is None else jnp.logical_and(ok, here)
        return ok

    def device(step):
        return {"gy": iy + step[0], "gz": iz + step[1]}

    loads[0].wait()
    loads[1].wait()
    flags = solid[:, 0, :].astype(F32)
    spread = (
        lax.broadcasted_iota(jnp.int32, (16, 128), 1) // 8 == lax.broadcasted_iota(jnp.int32, (16, 128), 0)
    ).astype(F32)
    solid_rows = jnp.dot(flags, spread, precision=HIGHEST, preferred_element_type=F32)
    for block in range(4):
        row = solid_rows[block : block + 1]
        for y in range(8 * block, 8 * block + 8):
            d = dens[y]
            mod[pl.ds(8 * (y + 1), 8), :] = row * (UNIT * MIN_MODULUS + (UNIT * (1.0 - MIN_MODULUS)) * (d * d * d))

    loads[2].wait()
    loads[3].wait()
    for c in range(3):
        def body(i, carry, c=c):
            for k in range(4):
                y = 4 * i + k
                r0[pl.ds(pl.multiple_of(256 * c + 8 * y, 8), 8), :] = jnp.where(fixed[y] != 0, 0.0, force[c, y])
            return carry
        lax.fori_loop(0, 8, body, 0)

    for side, y, moduli in ((0, 0, (0,)), (1, 31, (30, 31))):
        for c in range(3):
            first_y[side, c] = r0[pl.ds(256 * c + 8 * y, 8), :]
        for k, e in enumerate(moduli):
            first_y[side, 3 + k] = modulus(e + 1)
    for side, z, moduli in ((0, 0, (0,)), (1, 7, (6, 7))):
        for j in range(4):
            rows = pl.ds(8 * j, 8)
            for c in range(3):
                first_z[side, c, rows, :] = r0[pl.ds(256 * c + 64 * j + z, 8, 8), :]
            for k, e in enumerate(moduli):
                first_z[side, 3 + k, rows, :] = mod[pl.ds(64 * j + 8 + e, 8, 8), :]
    for i, (sy, sz) in enumerate(STEPS[4:]):
        for c in range(3):
            first_c[i, pl.ds(c, 1), :] = r0[pl.ds(256 * c + 8 * (0 if sy < 0 else 31) + (0 if sz < 0 else 7), 1), :]
        spots = [(y, z) for y in ((0,) if sy < 0 else (30, 31)) for z in ((0,) if sz < 0 else (6, 7))]
        for k, (y, z) in enumerate(spots):
            first_c[i, pl.ds(3 + k, 1), :] = mod[pl.ds(8 * (y + 1) + z, 1), :]

    pl.semaphore_wait(barrier, 8)

    def part_of(arrays, i):
        return arrays[0].at[i] if i < 2 else arrays[1].at[i - 2] if i < 4 else arrays[2].at[i - 4]

    seen = (seen_y, seen_z, seen_c)
    first_copies = [
        pltpu.make_async_remote_copy(
            part_of((first_y, first_z, first_c), i), part_of(seen, i), first_send.at[i], first_recv.at[i],
            device_id=device(step))
        for i, step in enumerate(STEPS)
    ]
    ORDER = (7, 6, 5, 4, 2, 3, 0, 1)
    for i in ORDER:
        @pl.when(there(STEPS[i]))
        def _(i=i):
            first_copies[i].start()
    greet(0)

    def away(i):
        return jnp.logical_not(there((-STEPS[i][0], -STEPS[i][1])))

    for i in range(8):
        @pl.when(away(i))
        def _(i=i):
            ref = part_of(seen, i)
            ref[...] = jnp.zeros(ref.shape, F32)

    rows_x = max(nz // 8, 1)
    cols_z = nz // rows_x

    def hops(i):
        dx, dz = i // cols_z, i % cols_z
        return -(min(dx, rows_x - dx) + min(dz, cols_z - dz))

    def other_z(i):
        x = lax.rem(iz // cols_z + i // cols_z, rows_x)
        return x * cols_z + lax.rem(iz + i % cols_z, cols_z)

    far_first = sorted(range(1, nz), key=hops)
    mine = pl.ds(pl.multiple_of(iz * 8, 8), 8)
    for i in range(lines):
        line_d[i, mine, :] = dens[iz * lines + i]

    for load in loads[4:]:
        load.wait()
    length = cosine.shape[0]
    gains = gain[...] * (1.0 / length)
    circ[...] = jnp.dot(cosine[...] * gains, cosine[...], precision=HIGHEST, preferred_element_type=F32) + jnp.dot(
        sine[...] * gains, sine[...], precision=HIGHEST, preferred_element_type=F32)

    def halo_copies(k, src, which):
        copies = []
        for i in which:
            sy, sz = STEPS[i]
            if sz == 0:
                s, d = src.at[:, pl.ds(PLANE * (1 if sy < 0 else 32), 8), :], land_y.at[k, i]
            elif sy == 0:
                s, d = stage_z.at[k, i - 2], land_z.at[k, i - 2]
            else:
                s, d = stage_c.at[k, i - 4], land_c.at[k, i - 4]
            copies.append((i, pltpu.make_async_remote_copy(
                s, d, halo_send.at[k, i], halo_recv.at[k, i], device_id=device(STEPS[i]))))
        return copies

    def send_halo(k, src, which):
        for c in range(3):
            for side, z in ((0, 0), (1, 7)):
                if side + 2 in which:
                    for j in range(4):
                        stage_z[k, side, c, pl.ds(8 * j, 8), :] = src[c, pl.ds(PLANE * (8 * j + 1) + z, 8, PLANE), :]
            for i in which:
                if i >= 4:
                    row = PLANE * (1 if STEPS[i][0] < 0 else 32) + (0 if STEPS[i][1] < 0 else 7)
                    stage_c[k, i - 4, pl.ds(c, 1), :] = src[c, pl.ds(row, 1), :]
        for i, copy in sorted(halo_copies(k, src, which), key=lambda item: ORDER.index(item[0])):
            @pl.when(there(STEPS[i]))
            def _(copy=copy):
                copy.start()

    def land_of(k, i):
        return land_y.at[k, i] if i < 2 else land_z.at[k, i - 2] if i < 4 else land_c.at[k, i - 4]

    def clear_halo(k, which):
        for i in which:
            @pl.when(jnp.logical_not(there((-STEPS[i][0], -STEPS[i][1]))))
            def _(i=i):
                ref = land_of(k, i)
                ref[...] = jnp.zeros(ref.shape, F32)

    def wait_halo(k, src, which):
        for i, copy in halo_copies(k, src, which):
            @pl.when(there((-STEPS[i][0], -STEPS[i][1])))
            def _(copy=copy):
                copy.wait_recv()

    def wait_sent(k, src, which):
        for i, copy in halo_copies(k, src, which):
            @pl.when(there(STEPS[i]))
            def _(copy=copy):
                copy.wait_send()

    def put(ref, vx, rows, u):
        ref[rows] = u
        vx[rows] = at_upper(u)

    def place_halo(k, ref, vx, which):
        for c in range(3):
            put(ref, vx, (c, pl.ds(PLANE * 33, 8), slice(None)), land_y[k, 0, c])
            if 1 in which:
                put(ref, vx, (c, pl.ds(0, 8), slice(None)), land_y[k, 1, c])
            for j in range(4):
                rows = (c, pl.ds(PLANE * (8 * j + 1) + 8, 8, PLANE), slice(None))
                put(ref, vx, rows, land_z[k, 0, c, pl.ds(8 * j, 8), :])
                if 3 in which:
                    u = land_z[k, 1, c, pl.ds(8 * j, 8), :]
                    low_z[c, pl.ds(8 * j + 1, 8), :] = u
                    low_zx[c, pl.ds(8 * j + 1, 8), :] = at_upper(u)
        for i in which:
            if i < 4:
                continue
            u = land_c[k, i - 4]
            ux = at_upper(u)
            y_row = 33 if STEPS[i][0] < 0 else 0
            for c in range(3):
                if STEPS[i][1] < 0:
                    ref[c, pl.ds(PLANE * y_row + 8, 1), :] = u[c : c + 1]
                    vx[c, pl.ds(PLANE * y_row + 8, 1), :] = ux[c : c + 1]
                else:
                    low_z[c, pl.ds(y_row, 1), :] = u[c : c + 1]
                    low_zx[c, pl.ds(y_row, 1), :] = ux[c : c + 1]

    def pair_zx(u0, x0, u1, x1):
        s0, d0, s1, d1 = u0 + x0, x0 - u0, u1 + x1, x1 - u1
        return {"00": s0 + s1, "01": d0 + d1, "10": s1 - s0, "11": d1 - d0}

    def plane(ref, vx, row):
        row = pl.multiple_of(row, PLANE)
        return [
            pair_zx(ref[c, pl.ds(row, 8), :], vx[c, pl.ds(row, 8), :], ref[c, pl.ds(row + 1, 8), :], vx[c, pl.ds(row + 1, 8), :])
            for c in range(3)
        ]

    def low_layer(ref, vx):
        for j in range(5):
            def rows(start):
                return [
                    pair_zx(
                        low_z[c, pl.ds(start, 8), :], low_zx[c, pl.ds(start, 8), :],
                        ref[c, pl.ds(PLANE * start, 8, PLANE), :], vx[c, pl.ds(PLANE * start, 8, PLANE), :])
                    for c in range(3)
                ]
            coefs = pair_y(rows(8 * j), rows(8 * j + 1))
            for c, g in enumerate(stress(*coefs, mod_z[pl.ds(8 * j + 1, 8), :])):
                for part, start, pa, pb in zip(spread_y(g), (8 * j, 8 * j + 1), (p_low, p_up), (q_low, q_up)):
                    s, d = part["00"] + part["10"], part["01"] + part["11"]
                    pa[c, pl.ds(start, 8), :] = s - d
                    pb[c, pl.ds(start, 8), :] = s + d
        for c in range(3):
            for j in range(4):
                rows = pl.ds(8 * j + 1, 8)
                to = (c, pl.ds(PLANE * 8 * j, 8, PLANE), slice(None))
                a_up[to] = p_low[c, rows, :] + p_up[c, rows, :]
                b_up[to] = q_low[c, rows, :] + q_up[c, rows, :]

    def flat(planes):
        return tuple(p[key] for p in planes for key in ("00", "01", "10", "11"))

    def unflat(values):
        keys = ("00", "01", "10", "11")
        return [dict(zip(keys, values[4 * c : 4 * c + 4])) for c in range(3)]

    def forces(ref, vx):
        low, high = plane(ref, vx, 0), plane(ref, vx, PLANE)
        upper = [spread_y(g)[1] for g in stress(*pair_y(low, high), modulus(0))]

        def one(e, low, upper):
            high = plane(ref, vx, PLANE * (e + 1))
            new = []
            for c, g in enumerate(stress(*pair_y(low, high), modulus(e))):
                lo, hi = spread_y(g)
                t = {key: upper[c][key] + lo[key] for key in lo}
                new.append(hi)
                sa, sb, da, db = t["00"] - t["01"], t["00"] + t["01"], t["10"] - t["11"], t["10"] + t["11"]
                row = pl.multiple_of(PLANE * (e - 1), PLANE)
                a_low[c, e - 1] = sa - da
                b_low[c, e - 1] = sb - db
                a_up[c, pl.ds(row + 1, 8), :] = sa + da
                b_up[c, pl.ds(row + 1, 8), :] = sb + db
            return high, new

        def body(i, carry):
            low, upper = unflat(carry[:12]), unflat(carry[12:])
            for k in range(4):
                low, upper = one(4 * i + 1 + k, low, upper)
            return flat(low) + flat(upper)

        lax.fori_loop(0, 8, body, flat(high) + flat(upper))

    def finish(ref, image, after, after_x):
        def body(i, carry):
            for k in range(4):
                y = 4 * i + k
                held = fixed[y] != 0
                scale = inv[y]
                row = pl.multiple_of(PLANE * y, PLANE)
                for c in range(3):
                    f = (a_low[c, y] + a_up[c, pl.ds(row, 8), :]) + from_lower(b_low[c, y] + b_up[c, pl.ds(row, 8), :])
                    v = ref[c, pl.ds(row + PLANE, 8), :]
                    w = jnp.where(held, v, f)
                    image[c, y] = w
                    new = scale * w - SHIFT * v
                    after[c, pl.ds(row + PLANE, 8), :] = new
                    after_x[c, pl.ds(row + PLANE, 8), :] = at_upper(new)
            return carry
        lax.fori_loop(0, 8, body, 0)

    def dots(pairs):
        def get(ref, c, y):
            if ref.shape[0] == 768:
                return ref[pl.ds(pl.multiple_of(256 * c + 8 * y, 8), 8), :]
            if ref.shape[1] == FAR:
                return ref[c, pl.ds(pl.multiple_of(PLANE * y + PLANE, PLANE), 8), :]
            return ref[c, y]

        def body(i, carry):
            carry = list(carry)
            for k in range(2):
                for c in range(3):
                    held = {}
                    for p, (slot, a, b) in enumerate(pairs):
                        for ref in (a, b):
                            if id(ref) not in held:
                                held[id(ref)] = get(ref, c, 2 * i + k)
                        carry[p] = carry[p] + held[id(a)] * held[id(b)]
            return tuple(carry)

        total = lax.fori_loop(0, 16, body, (zeros,) * len(pairs))
        for (slot, a, b), t in zip(pairs, total):
            acc[pl.ds(slot, 1), :] = jnp.sum(t, axis=0, keepdims=True)

    every = tuple(range(8))
    clear_halo(0, every)
    clear_halo(1, LOWERS)
    acc[...] = jnp.zeros(acc.shape, F32)

    for i in range(8):
        @pl.when(jnp.logical_not(away(i)))
        def _(i=i):
            first_copies[i].wait_recv()
    greeted(0)
    greet(1)

    mod[pl.ds(0, 8), :] = seen_y[1, 4]

    def row_of(u, k):
        return u[k : k + 1]

    low_low, up_low, low_up, up_up = seen_c[3], seen_c[1], seen_c[2], seen_c[0]
    for row, z1, z2, z7, z8 in (
        (0, row_of(low_low, 4), row_of(low_low, 3), row_of(seen_y[1, 3], 7), row_of(low_up, 3)),
        (1, row_of(low_low, 6), row_of(low_low, 5), row_of(seen_y[1, 4], 7), row_of(low_up, 4)),
        (34, row_of(up_low, 4), row_of(up_low, 3), row_of(seen_y[0, 3], 7), row_of(up_up, 3)),
    ):
        at = pl.ds(row, 1)
        mod_z[at, :] = z1
        sum_low[at, :] = z1 + z2
        sum_high[at, :] = z7 + z8
    for j in range(4):
        rows, to = pl.ds(8 * j, 8), pl.ds(8 * j + 2, 8)
        z1 = seen_z[1, 4, rows, :]
        mod_z[to, :] = z1
        sum_low[to, :] = z1 + seen_z[1, 3, rows, :]
        sum_high[to, :] = first_z[1, 4, rows, :] + seen_z[0, 3, rows, :]
    for c in range(3):
        for row, low, high in ((0, low_low, low_up), (33, up_low, up_up)):
            low_z[c, pl.ds(row, 1), :] = row_of(low, c)
            high_z[c, pl.ds(row, 1), :] = row_of(high, c)
        for j in range(4):
            rows, to = pl.ds(8 * j, 8), pl.ds(8 * j + 1, 8)
            low_z[c, to, :] = seen_z[1, c, rows, :]
            high_z[c, to, :] = seen_z[0, c, rows, :]

    def inverse_of(t):
        return 1.0 / jnp.maximum((KE_DIAG / UNIT) * (t + from_lower(t)), DIAG_FLOOR)

    for j in range(5):
        rows, above = pl.ds(8 * j, 8), pl.ds(8 * j + 1, 8)
        low_scale = inverse_of(sum_low[rows, :] + sum_low[above, :])
        high_scale = inverse_of(sum_high[rows, :] + sum_high[above, :])
        tmp[pl.ds(PLANE * 8 * j, 8, PLANE), :] = mod_z[rows, :] + mod_z[above, :]
        for c in range(3):
            u = low_scale * low_z[c, rows, :]
            low_z[c, rows, :] = u
            low_zx[c, rows, :] = at_upper(u)
            put(v0, x0, (c, pl.ds(PLANE * 8 * j + 8, 8, PLANE), slice(None)), high_scale * high_z[c, rows, :])

    def keep_sum(n, t):
        row = PLANE * n if isinstance(n, int) else pl.multiple_of(PLANE * n, PLANE)
        sums[n] = t
        tmp[pl.ds(row + 1, 8), :] = t

    def begin(n, loads_of):
        row = PLANE * n if isinstance(n, int) else pl.multiple_of(PLANE * n, PLANE)
        scale = inverse_of(sums[n] + tmp[pl.ds(row, 8), :])
        for c in range(3):
            put(v0, x0, (c, pl.ds(row, 8), slice(None)), scale * loads_of(c))
        return scale

    keep_sum(0, seen_y[1, 3] + seen_y[1, 4])
    keep_sum(33, modulus(32) + seen_y[0, 3])

    def sum_own(i, carry):
        for k in range(4):
            y = 4 * i + k
            keep_sum(y + 1, modulus(y) + modulus(y + 1))
        return carry
    lax.fori_loop(0, 8, sum_own, 0)
    begin(0, lambda c: seen_y[1, c])
    begin(33, lambda c: seen_y[0, c])

    def begin_own(i, carry):
        for k in range(4):
            y = 4 * i + k
            inv[y] = begin(y + 1, lambda c: r0[pl.ds(pl.multiple_of(256 * c + 8 * y, 8), 8), :])
        return carry
    lax.fori_loop(0, 8, begin_own, 0)

    low_layer(v0, x0)
    forces(v0, x0)
    finish(v0, w0, v1, x1)
    send_halo(0, v1, every)
    dots([(0, r0, v0), (1, r0, v1), (3, v0, w0), (4, v1, w0)])
    wait_halo(0, v1, every)
    greeted(1)
    greet(2)
    place_halo(0, v1, x1, every)
    low_layer(v1, x1)
    forces(v1, x1)
    finish(v1, w1, v2, x2)
    send_halo(1, v2, LOWERS)
    dots([(2, r0, v2), (5, v2, w0), (6, v1, w1), (7, v2, w1)])
    solid_scale = (-3.0 * (1.0 - MIN_MODULUS) * UNIT) * solid_rows
    for block in range(4):
        row = solid_scale[block : block + 1]
        for y in range(8 * block, 8 * block + 8):
            d = dens[y]
            weighted[y] = row * (d * d * d)
    wait_halo(1, v2, LOWERS)
    greeted(2)
    greet(3)
    place_halo(1, v2, x2, LOWERS)

    basis = ((v0, x0), (v1, x1), (v2, x2))

    def element_forms(chosen, pairs, with_total):
        def body(i, carry):
            lows = [unflat(carry[12 * k : 12 * k + 12]) for k in range(len(chosen))]
            for k in range(2):
                y = 2 * i + k
                highs = [plane(*basis[b], PLANE * (y + 2)) for b in chosen]
                coefs = {b: pair_y(low, high) for b, low, high in zip(chosen, lows, highs)}
                factor = weighted[y]
                for a in sorted({a for a, _ in pairs}):
                    pulled = stress(*coefs[a], 1.0)
                    for slot, (p, q) in enumerate(FORMS):
                        if (p, q) in pairs and p == a:
                            e = dot_forms(coefs[q], pulled)
                            forms[slot, y] = factor * e
                            if with_total:
                                carry = carry[:-1] + (carry[-1] + modulus(y + 1) * e,)
                lows = highs
            out = ()
            for low in lows:
                out = out + flat(low)
            return out + (carry[12 * len(chosen) :] if with_total else ())
        init = ()
        for b in chosen:
            init = init + flat(plane(*basis[b], PLANE))
        return lax.fori_loop(0, 16, body, init + ((zeros,) if with_total else ()))

    total = element_forms((2,), ((2, 2),), True)[-1]
    acc[pl.ds(8, 1), :] = jnp.sum(total, axis=0, keepdims=True)

    column = jnp.sum(acc[...], axis=1, keepdims=True)
    rows = lax.broadcasted_iota(jnp.int32, (16, 128), 0)
    lanes = lax.broadcasted_iota(jnp.int32, (16, 128), 1)
    part = jnp.sum(jnp.where(rows == lanes, column, 0.0), axis=0, keepdims=True)
    for k, (axis, me, n, slots) in enumerate((("gy", iy, ny, slots_y), ("gz", iz, nz, slots_z))):
        slots[me] = part

        if k == 1:
            greeted(3)
        far_y = sorted(range(1, ny), key=lambda i: -min(i, ny - i))
        for i in far_y if axis == "gy" else far_first:
            pltpu.make_async_remote_copy(
                slots.at[me], slots.at[me], sum_send.at[k], sum_recv.at[k],
                device_id={axis: lax.rem(me + i, n) if axis == "gy" else other_z(i)},
            ).start()
        if k == 0:
            element_forms((0, 1), ((0, 0), (0, 1), (1, 1)), False)
        else:
            for i in far_first:
                to = other_z(i)
                pltpu.make_async_remote_copy(
                    dens.at[pl.ds(to * lines, lines)], line_d.at[:, mine, :],
                    line_send.at[0], line_recv.at[0], device_id={"gz": to},
                ).start()
            element_forms((0, 1, 2), ((2, 0), (2, 1)), False)
        whole = slots.at[pl.ds(0, n - 1)]
        pltpu.make_async_copy(whole, whole, sum_recv.at[k]).wait()
        part = jnp.sum(slots[:, 0, :], axis=0, keepdims=True)

    lane1 = lax.broadcasted_iota(jnp.int32, (1, 128), 1)

    def entry(i):
        return jnp.sum(jnp.where(lane1 == i, part, 0.0), axis=1, keepdims=True)

    b0, b1, b2, g00, g10, g20, g11, g21, g22 = (entry(i) for i in range(9))
    l10, l20 = g10 / g00, g20 / g00
    d1 = g11 - l10 * g10
    e21 = g21 - l20 * g10
    l21 = e21 / d1
    d2 = g22 - l20 * g20 - l21 * e21
    y1 = b1 - l10 * b0
    y2 = b2 - l20 * b0 - l21 * y1
    c2 = y2 / d2
    c1 = y1 / d1 - l21 * c2
    c0 = b0 / g00 - l10 * c1 - l20 * c2
    wide = lambda c: jnp.broadcast_to(c, (8, 128))
    factors = [wide(c) for c in (c0 * c0, 2.0 * c0 * c1, c1 * c1, 2.0 * c2 * c0, 2.0 * c2 * c1, c2 * c2)]
    c0, c1, c2 = wide(c0), wide(c1), wide(c2)

    def weigh(i, carry):
        for k in range(4):
            y = 4 * i + k
            total = factors[0] * forms[0, y]
            for slot in range(1, 6):
                total = total + factors[slot] * forms[slot, y]
            weighted[y] = total
        return carry
    lax.fori_loop(0, 8, weigh, 0)

    for i in far_first:
        to = other_z(i)
        pltpu.make_async_remote_copy(
            weighted.at[pl.ds(to * lines, lines)], line_w.at[:, mine, :],
            line_send.at[1], line_recv.at[1], device_id={"gz": to},
        ).start()
    for i in range(lines):
        line_w[i, mine, :] = weighted[iz * lines + i]

    def displace(i, carry):
        for k in range(4):
            row = pl.multiple_of(PLANE * (4 * i + k + 1), PLANE)
            for c in range(3):
                rows = (c, pl.ds(row, 8), slice(None))
                disp[c, 4 * i + k] = c0 * v0[rows] + c1 * v1[rows] + c2 * v2[rows]
        return carry
    lax.fori_loop(0, 8, displace, 0)
    disp_copy = pltpu.make_async_copy(disp, disp_h, store_sem.at[0])
    disp_copy.start()

    others = [ref.at[:, pl.ds(0, 8 * (nz - 1)), :] for ref in (line_d, line_w)]
    for k in range(2):
        pltpu.make_async_copy(others[k], others[k], line_recv.at[k]).wait()
    for i in range(lines):
        back = jnp.dot(circ[...], line_w[i], precision=HIGHEST, preferred_element_type=F32)
        filt[i] = back / line_d[i]
    filt_copy = pltpu.make_async_copy(filt, filt_h, store_sem.at[1])
    filt_copy.start()

    for k in range(2):
        pltpu.make_async_copy(others[k], others[k], line_send.at[k]).wait()
    for k, (n, slots) in enumerate(((ny, slots_y), (nz, slots_z))):
        whole = slots.at[pl.ds(0, n - 1)]
        pltpu.make_async_copy(whole, whole, sum_send.at[k]).wait()
    for i in range(8):
        @pl.when(there(STEPS[i]))
        def _(i=i):
            first_copies[i].wait_send()
    wait_sent(0, v1, every)
    wait_sent(1, v2, LOWERS)
    disp_copy.wait()
    filt_copy.wait()


def settle(disp_h, filt_h, disp_o, filt_o, disp, filt, load_sem, store_sem):
    parts = [(disp_h.at[c], disp.at[c], disp_o.at[c]) for c in range(3)] + [(filt_h, filt, filt_o)]
    loads = [pltpu.make_async_copy(src, mid, load_sem.at[i]) for i, (src, mid, _) in enumerate(parts)]
    stores = [pltpu.make_async_copy(mid, dst, store_sem.at[i]) for i, (_, mid, dst) in enumerate(parts)]
    for load in loads:
        load.start()
    for load, store in zip(loads, stores):
        load.wait()
        store.start()
    for store in stores:
        store.wait()


def solution(mesh):
    ny, nz = mesh.shape["gy"], mesh.shape["gz"]
    lines = 32 // nz
    length = 8 * nz
    phases = np.outer(np.arange(length), np.arange(length)) % length
    cosine = np.cos(2.0 * np.pi / length * phases).astype(np.float32)
    sine = np.sin(2.0 * np.pi / length * phases).astype(np.float32)

    def local(force, density, solid_blocks, fixed_nodes, filter_gain):
        vmem = lambda *shape: pltpu.VMEM(shape, F32)
        dma = lambda *shape: pltpu.SemaphoreType.DMA(shape)
        node = [vmem(3, FAR, 128)]
        outs = pl.pallas_call(
            functools.partial(kernel, ny, nz, lines),
            out_shape=(
                jax.ShapeDtypeStruct((3, 32, 8, 128), F32),
                jax.ShapeDtypeStruct((lines, length, 128), F32),
            ),
            in_specs=[pl.BlockSpec(memory_space=pltpu.HBM)] * 7,
            out_specs=(pl.BlockSpec(memory_space=pltpu.HBM),) * 2,
            scratch_shapes=[
                vmem(3, 32, 8, 128), vmem(32, 8, 128), pltpu.VMEM((4, 1, 16), jnp.int32), pltpu.VMEM((32, 8, 128), jnp.int32),
                vmem(1, length), vmem(length, length), vmem(length, length),
                vmem(264, 128), vmem(48, 128), vmem(48, 128), vmem(48, 128), vmem(3, 48, 128),
                vmem(32, 8, 128), vmem(768, 128), vmem(3, 32, 8, 128), vmem(3, 32, 8, 128),
                *(node * 6), vmem(3, 48, 128), vmem(3, 48, 128),
                vmem(3, 32, 8, 128), vmem(3, 32, 8, 128), vmem(3, 640, 128), vmem(3, 640, 128),
                vmem(3, 48, 128), vmem(3, 48, 128), vmem(3, 48, 128), vmem(3, 48, 128),
                vmem(2, 5, 8, 128), vmem(2, 5, 32, 128), vmem(4, 8, 128),
                vmem(2, 5, 8, 128), vmem(2, 5, 32, 128), vmem(4, 8, 128),
                vmem(2, 2, 3, 32, 128), vmem(2, 4, 8, 128), vmem(2, 2, 3, 8, 128), vmem(2, 2, 3, 32, 128), vmem(2, 4, 8, 128),
                vmem(FAR, 128), vmem(34, 8, 128), vmem(16, 128), vmem(ny, 1, 128), vmem(nz, 1, 128), vmem(6, 32, 8, 128),
                vmem(length, length), vmem(32, 8, 128), vmem(lines, length, 128), vmem(lines, length, 128),
                vmem(3, 32, 8, 128), vmem(lines, length, 128),
                dma(7), dma(2), dma(8), dma(8), dma(2, 8), dma(2, 8), dma(2), dma(2), dma(2), dma(2),
                pltpu.SemaphoreType.REGULAR((2, 4)),
            ],
            compiler_params=pltpu.CompilerParams(collective_id=0, has_side_effects=True, vmem_limit_bytes=62 * 1024 * 1024),
            cost_estimate=pl.CostEstimate(flops=60_000_000, bytes_accessed=2_000_000, transcendentals=0),
        )(force, density, solid_blocks, fixed_nodes, filter_gain[None, :], jnp.asarray(cosine), jnp.asarray(sine))
        return pl.pallas_call(
            settle,
            out_shape=tuple(jax.ShapeDtypeStruct(x.shape, F32) for x in outs),
            in_specs=[pl.BlockSpec(memory_space=pltpu.HBM)] * 2,
            out_specs=(pl.BlockSpec(memory_space=pltpu.HBM),) * 2,
            scratch_shapes=[vmem(3, 32, 8, 128), vmem(lines, length, 128), dma(4), dma(4)],
            compiler_params=pltpu.CompilerParams(vmem_limit_bytes=62 * 1024 * 1024),
        )(*outs)

    in_specs = (P(None, "gy", "gz", None), P("gy", "gz", None), P("gy", "gz", None), P("gy", "gz", None), P())
    out_specs = (P(None, "gy", "gz", None), P(("gy", "gz"), None, None))
    return jax.shard_map(local, mesh=mesh, in_specs=in_specs, out_specs=out_specs, check_vma=False)
```

```python
import functools

import jax
import jax.numpy as jnp
import numpy as np
from jax import lax
from jax.experimental import pallas as pl
from jax.experimental.pallas import tpu as pltpu
from jax.sharding import PartitionSpec as P

MIN_MODULUS = 0.1
DIAG_FLOOR = 0.5
POISSON = 0.3
SHEAR = 1.0 / (2.0 * (1.0 + POISSON))
LAME = POISSON / ((1.0 + POISSON) * (1.0 - 2.0 * POISSON))
UNIT = SHEAR / 16.0
VOLUME = 0.5 * LAME / SHEAR
BEND = LAME / (3.0 * SHEAR)
TWIST = 1.0 / 3.0
WARP = (LAME + 4.0 * SHEAR) / 9.0 / SHEAR
KE_DIAG = (LAME + 4.0 * SHEAR) / 9.0
SHIFT = 1.0
PLANE = 16
FAR = 656
F32 = jnp.float32
HIGHEST = lax.Precision.HIGHEST
STEPS = [(-1, 0), (1, 0), (0, -1), (0, 1), (-1, -1), (-1, 1), (1, -1), (1, 1)]
LOWERS = (0, 2, 4)


def stress(y, z, x, m):
    m2, m3, m4 = 2.0 * m, TWIST * m, WARP * m
    gy, gz, gx = {}, {}, {}
    bulk = VOLUME * (y["100"] + z["010"] + x["001"])
    gy["100"] = m2 * (y["100"] + bulk)
    gz["010"] = m2 * (z["010"] + bulk)
    gx["001"] = m2 * (x["001"] + bulk)
    gy["010"] = gz["100"] = m * (y["010"] + z["100"])
    gz["001"] = gx["010"] = m * (z["001"] + x["010"])
    gy["001"] = gx["100"] = m * (y["001"] + x["100"])
    bend = BEND * (z["110"] + x["101"])
    gz["110"], gx["101"] = m * (z["110"] + bend), m * (x["101"] + bend)
    bend = BEND * (y["110"] + x["011"])
    gy["110"], gx["011"] = m * (y["110"] + bend), m * (x["011"] + bend)
    bend = BEND * (y["101"] + z["011"])
    gy["101"], gz["011"] = m * (y["101"] + bend), m * (z["011"] + bend)
    twist = y["011"] + z["101"] + x["110"]
    gy["011"] = m3 * (y["011"] + twist)
    gz["101"] = m3 * (z["101"] + twist)
    gx["110"] = m3 * (x["110"] + twist)
    gy["111"], gz["111"], gx["111"] = m4 * y["111"], m4 * z["111"], m4 * x["111"]
    return gy, gz, gx


FORMS = ((0, 0), (0, 1), (1, 1), (2, 0), (2, 1), (2, 2))


def dot_forms(coefs, pulled):
    total = None
    for c, g in zip(coefs, pulled):
        for key in g:
            term = c[key] * g[key]
            total = term if total is None else total + term
    return total


def pair_y(low, high):
    coefs = []
    for a, b in zip(low, high):
        c = {}
        for key in a:
            if key != "00":
                c["0" + key] = a[key] + b[key]
            c["1" + key] = b[key] - a[key]
        coefs.append(c)
    return coefs


def spread_y(g):
    low, high = {}, {}
    for key in ("00", "01", "10", "11"):
        d = g["1" + key]
        if key == "00":
            low[key], high[key] = -d, d
        else:
            s = g["0" + key]
            low[key], high[key] = s - d, s + d
    return low, high


def kernel(
    ny, nz, lines,
    force_h, dens_h, solid_h, fixed_h, gain_h, cos_h, sin_h,
    disp_h, filt_h,
    force, dens, solid, fixed, gain, cosine, sine,
    mod, mod_z, sum_low, sum_high, high_z,
    inv, r0, w0, w1, v0, v1, v2, x0, x1, x2, low_z, low_zx,
    a_low, b_low, a_up, b_up, p_low, p_up, q_low, q_up,
    first_y, first_z, first_c, seen_y, seen_z, seen_c,
    stage_z, stage_c, land_y, land_z, land_c,
    tmp, sums, acc, slots_y, slots_z, forms,
    circ, weighted, line_w, line_d, disp, filt,
    load_sem, store_sem, first_send, first_recv, halo_send, halo_recv, sum_send, sum_recv, line_send, line_recv, greet_sem,
):
    iy, iz = lax.axis_index("gy"), lax.axis_index("gz")
    lane = lax.broadcasted_iota(jnp.int32, (8, 128), 1)
    first_lane, last_lane = lane == 0, lane == 127
    zeros = jnp.zeros((8, 128), F32)

    def at_upper(u):
        return jnp.where(last_lane, 0.0, pltpu.roll(u, 127, 1))

    def from_lower(u):
        return jnp.where(first_lane, 0.0, pltpu.roll(u, 1, 1))

    def modulus(e):
        return mod[pl.ds(8 * e if isinstance(e, int) else pl.multiple_of(8 * e, 8), 8), :]

    loads = [
        pltpu.make_async_copy(src, dst, load_sem.at[i])
        for i, (src, dst) in enumerate(
            [(dens_h, dens), (solid_h, solid), (fixed_h, fixed), (force_h, force), (gain_h, gain), (cos_h, cosine), (sin_h, sine)]
        )
    ]
    for load in loads:
        load.start()

    barrier = pltpu.get_barrier_semaphore()

    def ring(sy, sz):
        return {"gy": lax.rem(iy + sy + ny, ny), "gz": lax.rem(iz + sz + nz, nz)}

    for sy, sz in STEPS:
        pl.semaphore_signal(barrier, 1, device_id=ring(sy, sz))

    def greeters(r):
        return [(a, axis, n) for a, (axis, n) in enumerate((("gy", ny), ("gz", nz))) if n >= 4 << r]

    def greet(r):
        for a, axis, n in greeters(r):
            for d in (1 << r, n - (1 << r)):
                to = lax.rem((iy if axis == "gy" else iz) + d, n)
                pl.semaphore_signal(greet_sem.at[a, r], 1, device_id={axis: to})

    def greeted(r):
        for a, axis, n in greeters(r):
            pl.semaphore_wait(greet_sem.at[a, r], 2)

    def there(step):
        sy, sz = step
        ok = None
        for index, s, n in ((iy, sy, ny), (iz, sz, nz)):
            if s:
                here = index >= 1 if s < 0 else index < n - 1
                ok = here if ok is None else jnp.logical_and(ok, here)
        return ok

    def device(step):
        return {"gy": iy + step[0], "gz": iz + step[1]}

    loads[0].wait()
    loads[1].wait()
    flags = solid[:, 0, :].astype(F32)
    spread = (
        lax.broadcasted_iota(jnp.int32, (16, 128), 1) // 8 == lax.broadcasted_iota(jnp.int32, (16, 128), 0)
    ).astype(F32)
    solid_rows = jnp.dot(flags, spread, precision=HIGHEST, preferred_element_type=F32)
    for block in range(4):
        row = solid_rows[block : block + 1]
        for y in range(8 * block, 8 * block + 8):
            d = dens[y]
            mod[pl.ds(8 * (y + 1), 8), :] = row * (UNIT * MIN_MODULUS + (UNIT * (1.0 - MIN_MODULUS)) * (d * d * d))

    loads[2].wait()
    loads[3].wait()
    for c in range(3):
        def body(i, carry, c=c):
            for k in range(4):
                y = 4 * i + k
                r0[pl.ds(pl.multiple_of(256 * c + 8 * y, 8), 8), :] = jnp.where(fixed[y] != 0, 0.0, force[c, y])
            return carry
        lax.fori_loop(0, 8, body, 0)

    for side, y, moduli in ((0, 0, (0,)), (1, 31, (30, 31))):
        for c in range(3):
            first_y[side, c] = r0[pl.ds(256 * c + 8 * y, 8), :]
        for k, e in enumerate(moduli):
            first_y[side, 3 + k] = modulus(e + 1)
    for side, z, moduli in ((0, 0, (0,)), (1, 7, (6, 7))):
        for j in range(4):
            rows = pl.ds(8 * j, 8)
            for c in range(3):
                first_z[side, c, rows, :] = r0[pl.ds(256 * c + 64 * j + z, 8, 8), :]
            for k, e in enumerate(moduli):
                first_z[side, 3 + k, rows, :] = mod[pl.ds(64 * j + 8 + e, 8, 8), :]
    for i, (sy, sz) in enumerate(STEPS[4:]):
        for c in range(3):
            first_c[i, pl.ds(c, 1), :] = r0[pl.ds(256 * c + 8 * (0 if sy < 0 else 31) + (0 if sz < 0 else 7), 1), :]
        spots = [(y, z) for y in ((0,) if sy < 0 else (30, 31)) for z in ((0,) if sz < 0 else (6, 7))]
        for k, (y, z) in enumerate(spots):
            first_c[i, pl.ds(3 + k, 1), :] = mod[pl.ds(8 * (y + 1) + z, 1), :]

    pl.semaphore_wait(barrier, 8)

    def part_of(arrays, i):
        return arrays[0].at[i] if i < 2 else arrays[1].at[i - 2] if i < 4 else arrays[2].at[i - 4]

    seen = (seen_y, seen_z, seen_c)
    first_copies = [
        pltpu.make_async_remote_copy(
            part_of((first_y, first_z, first_c), i), part_of(seen, i), first_send.at[i], first_recv.at[i],
            device_id=device(step))
        for i, step in enumerate(STEPS)
    ]
    ORDER = (7, 6, 5, 4, 2, 3, 0, 1)
    for i in ORDER:
        @pl.when(there(STEPS[i]))
        def _(i=i):
            first_copies[i].start()
    greet(0)

    def away(i):
        return jnp.logical_not(there((-STEPS[i][0], -STEPS[i][1])))

    for i in range(8):
        @pl.when(away(i))
        def _(i=i):
            ref = part_of(seen, i)
            ref[...] = jnp.zeros(ref.shape, F32)

    rows_x = max(nz // 8, 1)
    cols_z = nz // rows_x

    def hops(i):
        dx, dz = i // cols_z, i % cols_z
        return -(min(dx, rows_x - dx) + min(dz, cols_z - dz))

    def other_z(i):
        x = lax.rem(iz // cols_z + i // cols_z, rows_x)
        return x * cols_z + lax.rem(iz + i % cols_z, cols_z)

    far_first = sorted(range(1, nz), key=hops)
    mine = pl.ds(pl.multiple_of(iz * 8, 8), 8)
    for i in range(lines):
        line_d[i, mine, :] = dens[iz * lines + i]

    for load in loads[4:]:
        load.wait()
    length = cosine.shape[0]
    gains = gain[...] * (1.0 / length)
    circ[...] = jnp.dot(cosine[...] * gains, cosine[...], precision=HIGHEST, preferred_element_type=F32) + jnp.dot(
        sine[...] * gains, sine[...], precision=HIGHEST, preferred_element_type=F32)

    def halo_copies(k, src, which):
        copies = []
        for i in which:
            sy, sz = STEPS[i]
            if sz == 0:
                s, d = src.at[:, pl.ds(PLANE * (1 if sy < 0 else 32), 8), :], land_y.at[k, i]
            elif sy == 0:
                s, d = stage_z.at[k, i - 2], land_z.at[k, i - 2]
            else:
                s, d = stage_c.at[k, i - 4], land_c.at[k, i - 4]
            copies.append((i, pltpu.make_async_remote_copy(
                s, d, halo_send.at[k, i], halo_recv.at[k, i], device_id=device(STEPS[i]))))
        return copies

    def send_halo(k, src, which):
        for c in range(3):
            for side, z in ((0, 0), (1, 7)):
                if side + 2 in which:
                    for j in range(4):
                        stage_z[k, side, c, pl.ds(8 * j, 8), :] = src[c, pl.ds(PLANE * (8 * j + 1) + z, 8, PLANE), :]
            for i in which:
                if i >= 4:
                    row = PLANE * (1 if STEPS[i][0] < 0 else 32) + (0 if STEPS[i][1] < 0 else 7)
                    stage_c[k, i - 4, pl.ds(c, 1), :] = src[c, pl.ds(row, 1), :]
        for i, copy in sorted(halo_copies(k, src, which), key=lambda item: ORDER.index(item[0])):
            @pl.when(there(STEPS[i]))
            def _(copy=copy):
                copy.start()

    def land_of(k, i):
        return land_y.at[k, i] if i < 2 else land_z.at[k, i - 2] if i < 4 else land_c.at[k, i - 4]

    def clear_halo(k, which):
        for i in which:
            @pl.when(jnp.logical_not(there((-STEPS[i][0], -STEPS[i][1]))))
            def _(i=i):
                ref = land_of(k, i)
                ref[...] = jnp.zeros(ref.shape, F32)

    def wait_halo(k, src, which):
        for i, copy in halo_copies(k, src, which):
            @pl.when(there((-STEPS[i][0], -STEPS[i][1])))
            def _(copy=copy):
                copy.wait_recv()

    def wait_sent(k, src, which):
        for i, copy in halo_copies(k, src, which):
            @pl.when(there(STEPS[i]))
            def _(copy=copy):
                copy.wait_send()

    def put(ref, vx, rows, u):
        ref[rows] = u
        vx[rows] = at_upper(u)

    def place_halo(k, ref, vx, which):
        for c in range(3):
            put(ref, vx, (c, pl.ds(PLANE * 33, 8), slice(None)), land_y[k, 0, c])
            if 1 in which:
                put(ref, vx, (c, pl.ds(0, 8), slice(None)), land_y[k, 1, c])
            for j in range(4):
                rows = (c, pl.ds(PLANE * (8 * j + 1) + 8, 8, PLANE), slice(None))
                put(ref, vx, rows, land_z[k, 0, c, pl.ds(8 * j, 8), :])
                if 3 in which:
                    u = land_z[k, 1, c, pl.ds(8 * j, 8), :]
                    low_z[c, pl.ds(8 * j + 1, 8), :] = u
                    low_zx[c, pl.ds(8 * j + 1, 8), :] = at_upper(u)
        for i in which:
            if i < 4:
                continue
            u = land_c[k, i - 4]
            ux = at_upper(u)
            y_row = 33 if STEPS[i][0] < 0 else 0
            for c in range(3):
                if STEPS[i][1] < 0:
                    ref[c, pl.ds(PLANE * y_row + 8, 1), :] = u[c : c + 1]
                    vx[c, pl.ds(PLANE * y_row + 8, 1), :] = ux[c : c + 1]
                else:
                    low_z[c, pl.ds(y_row, 1), :] = u[c : c + 1]
                    low_zx[c, pl.ds(y_row, 1), :] = ux[c : c + 1]

    def pair_zx(u0, x0, u1, x1):
        s0, d0, s1, d1 = u0 + x0, x0 - u0, u1 + x1, x1 - u1
        return {"00": s0 + s1, "01": d0 + d1, "10": s1 - s0, "11": d1 - d0}

    def plane(ref, vx, row):
        row = pl.multiple_of(row, PLANE)
        return [
            pair_zx(ref[c, pl.ds(row, 8), :], vx[c, pl.ds(row, 8), :], ref[c, pl.ds(row + 1, 8), :], vx[c, pl.ds(row + 1, 8), :])
            for c in range(3)
        ]

    def low_layer(ref, vx):
        for j in range(5):
            def rows(start):
                return [
                    pair_zx(
                        low_z[c, pl.ds(start, 8), :], low_zx[c, pl.ds(start, 8), :],
                        ref[c, pl.ds(PLANE * start, 8, PLANE), :], vx[c, pl.ds(PLANE * start, 8, PLANE), :])
                    for c in range(3)
                ]
            coefs = pair_y(rows(8 * j), rows(8 * j + 1))
            for c, g in enumerate(stress(*coefs, mod_z[pl.ds(8 * j + 1, 8), :])):
                for part, start, pa, pb in zip(spread_y(g), (8 * j, 8 * j + 1), (p_low, p_up), (q_low, q_up)):
                    s, d = part["00"] + part["10"], part["01"] + part["11"]
                    pa[c, pl.ds(start, 8), :] = s - d
                    pb[c, pl.ds(start, 8), :] = s + d
        for c in range(3):
            for j in range(4):
                rows = pl.ds(8 * j + 1, 8)
                to = (c, pl.ds(PLANE * 8 * j, 8, PLANE), slice(None))
                a_up[to] = p_low[c, rows, :] + p_up[c, rows, :]
                b_up[to] = q_low[c, rows, :] + q_up[c, rows, :]

    def flat(planes):
        return tuple(p[key] for p in planes for key in ("00", "01", "10", "11"))

    def unflat(values):
        keys = ("00", "01", "10", "11")
        return [dict(zip(keys, values[4 * c : 4 * c + 4])) for c in range(3)]

    def forces(ref, vx):
        low, high = plane(ref, vx, 0), plane(ref, vx, PLANE)
        upper = [spread_y(g)[1] for g in stress(*pair_y(low, high), modulus(0))]

        def one(e, low, upper):
            high = plane(ref, vx, PLANE * (e + 1))
            new = []
            for c, g in enumerate(stress(*pair_y(low, high), modulus(e))):
                lo, hi = spread_y(g)
                t = {key: upper[c][key] + lo[key] for key in lo}
                new.append(hi)
                sa, sb, da, db = t["00"] - t["01"], t["00"] + t["01"], t["10"] - t["11"], t["10"] + t["11"]
                row = pl.multiple_of(PLANE * (e - 1), PLANE)
                a_low[c, e - 1] = sa - da
                b_low[c, e - 1] = sb - db
                a_up[c, pl.ds(row + 1, 8), :] = sa + da
                b_up[c, pl.ds(row + 1, 8), :] = sb + db
            return high, new

        def body(i, carry):
            low, upper = unflat(carry[:12]), unflat(carry[12:])
            for k in range(4):
                low, upper = one(4 * i + 1 + k, low, upper)
            return flat(low) + flat(upper)

        lax.fori_loop(0, 8, body, flat(high) + flat(upper))

    def finish(ref, image, after, after_x):
        def body(i, carry):
            for k in range(16):
                y = 16 * i + k
                held = fixed[y] != 0
                scale = inv[y]
                row = pl.multiple_of(PLANE * y, PLANE)
                for c in range(3):
                    f = (a_low[c, y] + a_up[c, pl.ds(row, 8), :]) + from_lower(b_low[c, y] + b_up[c, pl.ds(row, 8), :])
                    v = ref[c, pl.ds(row + PLANE, 8), :]
                    w = jnp.where(held, v, f)
                    image[c, y] = w
                    new = scale * w - SHIFT * v
                    after[c, pl.ds(row + PLANE, 8), :] = new
                    after_x[c, pl.ds(row + PLANE, 8), :] = at_upper(new)
            return carry
        lax.fori_loop(0, 2, body, 0)

    def dots(pairs):
        def get(ref, c, y):
            if ref.shape[0] == 768:
                return ref[pl.ds(pl.multiple_of(256 * c + 8 * y, 8), 8), :]
            if ref.shape[1] == FAR:
                return ref[c, pl.ds(pl.multiple_of(PLANE * y + PLANE, PLANE), 8), :]
            return ref[c, y]

        def body(i, carry):
            carry = list(carry)
            for k in range(2):
                for c in range(3):
                    held = {}
                    for p, (slot, a, b) in enumerate(pairs):
                        for ref in (a, b):
                            if id(ref) not in held:
                                held[id(ref)] = get(ref, c, 2 * i + k)
                        carry[p] = carry[p] + held[id(a)] * held[id(b)]
            return tuple(carry)

        total = lax.fori_loop(0, 16, body, (zeros,) * len(pairs))
        for (slot, a, b), t in zip(pairs, total):
            acc[pl.ds(slot, 1), :] = jnp.sum(t, axis=0, keepdims=True)

    every = tuple(range(8))
    clear_halo(0, every)
    clear_halo(1, LOWERS)
    acc[...] = jnp.zeros(acc.shape, F32)

    for i in range(8):
        @pl.when(jnp.logical_not(away(i)))
        def _(i=i):
            first_copies[i].wait_recv()
    greeted(0)
    greet(1)

    mod[pl.ds(0, 8), :] = seen_y[1, 4]

    def row_of(u, k):
        return u[k : k + 1]

    low_low, up_low, low_up, up_up = seen_c[3], seen_c[1], seen_c[2], seen_c[0]
    for row, z1, z2, z7, z8 in (
        (0, row_of(low_low, 4), row_of(low_low, 3), row_of(seen_y[1, 3], 7), row_of(low_up, 3)),
        (1, row_of(low_low, 6), row_of(low_low, 5), row_of(seen_y[1, 4], 7), row_of(low_up, 4)),
        (34, row_of(up_low, 4), row_of(up_low, 3), row_of(seen_y[0, 3], 7), row_of(up_up, 3)),
    ):
        at = pl.ds(row, 1)
        mod_z[at, :] = z1
        sum_low[at, :] = z1 + z2
        sum_high[at, :] = z7 + z8
    for j in range(4):
        rows, to = pl.ds(8 * j, 8), pl.ds(8 * j + 2, 8)
        z1 = seen_z[1, 4, rows, :]
        mod_z[to, :] = z1
        sum_low[to, :] = z1 + seen_z[1, 3, rows, :]
        sum_high[to, :] = first_z[1, 4, rows, :] + seen_z[0, 3, rows, :]
    for c in range(3):
        for row, low, high in ((0, low_low, low_up), (33, up_low, up_up)):
            low_z[c, pl.ds(row, 1), :] = row_of(low, c)
            high_z[c, pl.ds(row, 1), :] = row_of(high, c)
        for j in range(4):
            rows, to = pl.ds(8 * j, 8), pl.ds(8 * j + 1, 8)
            low_z[c, to, :] = seen_z[1, c, rows, :]
            high_z[c, to, :] = seen_z[0, c, rows, :]

    def inverse_of(t):
        return 1.0 / jnp.maximum((KE_DIAG / UNIT) * (t + from_lower(t)), DIAG_FLOOR)

    for j in range(5):
        rows, above = pl.ds(8 * j, 8), pl.ds(8 * j + 1, 8)
        low_scale = inverse_of(sum_low[rows, :] + sum_low[above, :])
        high_scale = inverse_of(sum_high[rows, :] + sum_high[above, :])
        tmp[pl.ds(PLANE * 8 * j, 8, PLANE), :] = mod_z[rows, :] + mod_z[above, :]
        for c in range(3):
            u = low_scale * low_z[c, rows, :]
            low_z[c, rows, :] = u
            low_zx[c, rows, :] = at_upper(u)
            put(v0, x0, (c, pl.ds(PLANE * 8 * j + 8, 8, PLANE), slice(None)), high_scale * high_z[c, rows, :])

    def keep_sum(n, t):
        row = PLANE * n if isinstance(n, int) else pl.multiple_of(PLANE * n, PLANE)
        sums[n] = t
        tmp[pl.ds(row + 1, 8), :] = t

    def begin(n, loads_of):
        row = PLANE * n if isinstance(n, int) else pl.multiple_of(PLANE * n, PLANE)
        scale = inverse_of(sums[n] + tmp[pl.ds(row, 8), :])
        for c in range(3):
            put(v0, x0, (c, pl.ds(row, 8), slice(None)), scale * loads_of(c))
        return scale

    keep_sum(0, seen_y[1, 3] + seen_y[1, 4])
    keep_sum(33, modulus(32) + seen_y[0, 3])

    def sum_own(i, carry):
        for k in range(4):
            y = 4 * i + k
            keep_sum(y + 1, modulus(y) + modulus(y + 1))
        return carry
    lax.fori_loop(0, 8, sum_own, 0)
    begin(0, lambda c: seen_y[1, c])
    begin(33, lambda c: seen_y[0, c])

    def begin_own(i, carry):
        for k in range(8):
            y = 8 * i + k
            inv[y] = begin(y + 1, lambda c: r0[pl.ds(pl.multiple_of(256 * c + 8 * y, 8), 8), :])
        return carry
    lax.fori_loop(0, 4, begin_own, 0)

    low_layer(v0, x0)
    forces(v0, x0)
    finish(v0, w0, v1, x1)
    send_halo(0, v1, every)
    dots([(0, r0, v0), (1, r0, v1), (3, v0, w0), (4, v1, w0)])
    wait_halo(0, v1, every)
    greeted(1)
    greet(2)
    place_halo(0, v1, x1, every)
    low_layer(v1, x1)
    forces(v1, x1)
    finish(v1, w1, v2, x2)
    send_halo(1, v2, LOWERS)
    dots([(2, r0, v2), (5, v2, w0), (6, v1, w1), (7, v2, w1)])
    solid_scale = (-3.0 * (1.0 - MIN_MODULUS) * UNIT) * solid_rows
    for block in range(4):
        row = solid_scale[block : block + 1]
        for y in range(8 * block, 8 * block + 8):
            d = dens[y]
            weighted[y] = row * (d * d * d)
    wait_halo(1, v2, LOWERS)
    greeted(2)
    greet(3)
    place_halo(1, v2, x2, LOWERS)

    basis = ((v0, x0), (v1, x1), (v2, x2))

    def element_forms(chosen, pairs, with_total):
        def body(i, carry):
            lows = [unflat(carry[12 * k : 12 * k + 12]) for k in range(len(chosen))]
            for k in range(2):
                y = 2 * i + k
                highs = [plane(*basis[b], PLANE * (y + 2)) for b in chosen]
                coefs = {b: pair_y(low, high) for b, low, high in zip(chosen, lows, highs)}
                factor = weighted[y]
                for a in sorted({a for a, _ in pairs}):
                    pulled = stress(*coefs[a], 1.0)
                    for slot, (p, q) in enumerate(FORMS):
                        if (p, q) in pairs and p == a:
                            e = dot_forms(coefs[q], pulled)
                            forms[slot, y] = factor * e
                            if with_total:
                                carry = carry[:-1] + (carry[-1] + modulus(y + 1) * e,)
                lows = highs
            out = ()
            for low in lows:
                out = out + flat(low)
            return out + (carry[12 * len(chosen) :] if with_total else ())
        init = ()
        for b in chosen:
            init = init + flat(plane(*basis[b], PLANE))
        return lax.fori_loop(0, 16, body, init + ((zeros,) if with_total else ()))

    total = element_forms((2,), ((2, 2),), True)[-1]
    acc[pl.ds(8, 1), :] = jnp.sum(total, axis=0, keepdims=True)

    column = jnp.sum(acc[...], axis=1, keepdims=True)
    rows = lax.broadcasted_iota(jnp.int32, (16, 128), 0)
    lanes = lax.broadcasted_iota(jnp.int32, (16, 128), 1)
    part = jnp.sum(jnp.where(rows == lanes, column, 0.0), axis=0, keepdims=True)
    for k, (axis, me, n, slots) in enumerate((("gy", iy, ny, slots_y), ("gz", iz, nz, slots_z))):
        slots[me] = part

        if k == 1:
            greeted(3)
        far_y = sorted(range(1, ny), key=lambda i: -min(i, ny - i))
        for i in far_y if axis == "gy" else far_first:
            pltpu.make_async_remote_copy(
                slots.at[me], slots.at[me], sum_send.at[k], sum_recv.at[k],
                device_id={axis: lax.rem(me + i, n) if axis == "gy" else other_z(i)},
            ).start()
        if k == 0:
            element_forms((0, 1), ((0, 0), (0, 1), (1, 1)), False)
        else:
            for i in far_first:
                to = other_z(i)
                pltpu.make_async_remote_copy(
                    dens.at[pl.ds(to * lines, lines)], line_d.at[:, mine, :],
                    line_send.at[0], line_recv.at[0], device_id={"gz": to},
                ).start()
            element_forms((0, 1, 2), ((2, 0), (2, 1)), False)
        whole = slots.at[pl.ds(0, n - 1)]
        pltpu.make_async_copy(whole, whole, sum_recv.at[k]).wait()
        part = jnp.sum(slots[:, 0, :], axis=0, keepdims=True)

    lane1 = lax.broadcasted_iota(jnp.int32, (1, 128), 1)

    def entry(i):
        return jnp.sum(jnp.where(lane1 == i, part, 0.0), axis=1, keepdims=True)

    b0, b1, b2, g00, g10, g20, g11, g21, g22 = (entry(i) for i in range(9))
    l10, l20 = g10 / g00, g20 / g00
    d1 = g11 - l10 * g10
    e21 = g21 - l20 * g10
    l21 = e21 / d1
    d2 = g22 - l20 * g20 - l21 * e21
    y1 = b1 - l10 * b0
    y2 = b2 - l20 * b0 - l21 * y1
    c2 = y2 / d2
    c1 = y1 / d1 - l21 * c2
    c0 = b0 / g00 - l10 * c1 - l20 * c2
    wide = lambda c: jnp.broadcast_to(c, (8, 128))
    factors = [wide(c) for c in (c0 * c0, 2.0 * c0 * c1, c1 * c1, 2.0 * c2 * c0, 2.0 * c2 * c1, c2 * c2)]
    c0, c1, c2 = wide(c0), wide(c1), wide(c2)

    def weigh(i, carry):
        for k in range(4):
            y = 4 * i + k
            total = factors[0] * forms[0, y]
            for slot in range(1, 6):
                total = total + factors[slot] * forms[slot, y]
            weighted[y] = total
        return carry
    lax.fori_loop(0, 8, weigh, 0)

    for i in far_first:
        to = other_z(i)
        pltpu.make_async_remote_copy(
            weighted.at[pl.ds(to * lines, lines)], line_w.at[:, mine, :],
            line_send.at[1], line_recv.at[1], device_id={"gz": to},
        ).start()
    for i in range(lines):
        line_w[i, mine, :] = weighted[iz * lines + i]

    def displace(i, carry):
        for k in range(4):
            row = pl.multiple_of(PLANE * (4 * i + k + 1), PLANE)
            for c in range(3):
                rows = (c, pl.ds(row, 8), slice(None))
                disp[c, 4 * i + k] = c0 * v0[rows] + c1 * v1[rows] + c2 * v2[rows]
        return carry
    lax.fori_loop(0, 8, displace, 0)
    disp_copy = pltpu.make_async_copy(disp, disp_h, store_sem.at[0])
    disp_copy.start()

    others = [ref.at[:, pl.ds(0, 8 * (nz - 1)), :] for ref in (line_d, line_w)]
    for k in range(2):
        pltpu.make_async_copy(others[k], others[k], line_recv.at[k]).wait()
    for i in range(lines):
        back = jnp.dot(circ[...], line_w[i], precision=HIGHEST, preferred_element_type=F32)
        filt[i] = back / line_d[i]
    filt_copy = pltpu.make_async_copy(filt, filt_h, store_sem.at[1])
    filt_copy.start()

    for k in range(2):
        pltpu.make_async_copy(others[k], others[k], line_send.at[k]).wait()
    for k, (n, slots) in enumerate(((ny, slots_y), (nz, slots_z))):
        whole = slots.at[pl.ds(0, n - 1)]
        pltpu.make_async_copy(whole, whole, sum_send.at[k]).wait()
    for i in range(8):
        @pl.when(there(STEPS[i]))
        def _(i=i):
            first_copies[i].wait_send()
    wait_sent(0, v1, every)
    wait_sent(1, v2, LOWERS)
    disp_copy.wait()
    filt_copy.wait()


def settle(disp_h, filt_h, disp_o, filt_o, disp, filt, load_sem, store_sem):
    parts = [(disp_h.at[c], disp.at[c], disp_o.at[c]) for c in range(3)] + [(filt_h, filt, filt_o)]
    loads = [pltpu.make_async_copy(src, mid, load_sem.at[i]) for i, (src, mid, _) in enumerate(parts)]
    stores = [pltpu.make_async_copy(mid, dst, store_sem.at[i]) for i, (_, mid, dst) in enumerate(parts)]
    for load in loads:
        load.start()
    for load, store in zip(loads, stores):
        load.wait()
        store.start()
    for store in stores:
        store.wait()


def solution(mesh):
    ny, nz = mesh.shape["gy"], mesh.shape["gz"]
    lines = 32 // nz
    length = 8 * nz
    phases = np.outer(np.arange(length), np.arange(length)) % length
    cosine = np.cos(2.0 * np.pi / length * phases).astype(np.float32)
    sine = np.sin(2.0 * np.pi / length * phases).astype(np.float32)

    def local(force, density, solid_blocks, fixed_nodes, filter_gain):
        vmem = lambda *shape: pltpu.VMEM(shape, F32)
        dma = lambda *shape: pltpu.SemaphoreType.DMA(shape)
        node = [vmem(3, FAR, 128)]
        outs = pl.pallas_call(
            functools.partial(kernel, ny, nz, lines),
            out_shape=(
                jax.ShapeDtypeStruct((3, 32, 8, 128), F32),
                jax.ShapeDtypeStruct((lines, length, 128), F32),
            ),
            in_specs=[pl.BlockSpec(memory_space=pltpu.HBM)] * 7,
            out_specs=(pl.BlockSpec(memory_space=pltpu.HBM),) * 2,
            scratch_shapes=[
                vmem(3, 32, 8, 128), vmem(32, 8, 128), pltpu.VMEM((4, 1, 16), jnp.int32), pltpu.VMEM((32, 8, 128), jnp.int32),
                vmem(1, length), vmem(length, length), vmem(length, length),
                vmem(264, 128), vmem(48, 128), vmem(48, 128), vmem(48, 128), vmem(3, 48, 128),
                vmem(32, 8, 128), vmem(768, 128), vmem(3, 32, 8, 128), vmem(3, 32, 8, 128),
                *(node * 6), vmem(3, 48, 128), vmem(3, 48, 128),
                vmem(3, 32, 8, 128), vmem(3, 32, 8, 128), vmem(3, 640, 128), vmem(3, 640, 128),
                vmem(3, 48, 128), vmem(3, 48, 128), vmem(3, 48, 128), vmem(3, 48, 128),
                vmem(2, 5, 8, 128), vmem(2, 5, 32, 128), vmem(4, 8, 128),
                vmem(2, 5, 8, 128), vmem(2, 5, 32, 128), vmem(4, 8, 128),
                vmem(2, 2, 3, 32, 128), vmem(2, 4, 8, 128), vmem(2, 2, 3, 8, 128), vmem(2, 2, 3, 32, 128), vmem(2, 4, 8, 128),
                vmem(FAR, 128), vmem(34, 8, 128), vmem(16, 128), vmem(ny, 1, 128), vmem(nz, 1, 128), vmem(6, 32, 8, 128),
                vmem(length, length), vmem(32, 8, 128), vmem(lines, length, 128), vmem(lines, length, 128),
                vmem(3, 32, 8, 128), vmem(lines, length, 128),
                dma(7), dma(2), dma(8), dma(8), dma(2, 8), dma(2, 8), dma(2), dma(2), dma(2), dma(2),
                pltpu.SemaphoreType.REGULAR((2, 4)),
            ],
            compiler_params=pltpu.CompilerParams(collective_id=0, has_side_effects=True, vmem_limit_bytes=62 * 1024 * 1024),
            cost_estimate=pl.CostEstimate(flops=60_000_000, bytes_accessed=2_000_000, transcendentals=0),
        )(force, density, solid_blocks, fixed_nodes, filter_gain[None, :], jnp.asarray(cosine), jnp.asarray(sine))
        return pl.pallas_call(
            settle,
            out_shape=tuple(jax.ShapeDtypeStruct(x.shape, F32) for x in outs),
            in_specs=[pl.BlockSpec(memory_space=pltpu.HBM)] * 2,
            out_specs=(pl.BlockSpec(memory_space=pltpu.HBM),) * 2,
            scratch_shapes=[vmem(3, 32, 8, 128), vmem(lines, length, 128), dma(4), dma(4)],
            compiler_params=pltpu.CompilerParams(vmem_limit_bytes=62 * 1024 * 1024),
        )(*outs)

    in_specs = (P(None, "gy", "gz", None), P("gy", "gz", None), P("gy", "gz", None), P("gy", "gz", None), P())
    out_specs = (P(None, "gy", "gz", None), P(("gy", "gz"), None, None))
    return jax.shard_map(local, mesh=mesh, in_specs=in_specs, out_specs=out_specs, check_vma=False)
```
